128 devices in a mesh: st: 16 (over y, x), fq: 8 (over z, core).
Axes of the slice: x: 4, y: 4, z: 4, core: 2. Of those that a mesh axis runs over, the one named last changes fastest.
Arguments:
- signals: bfloat16 [1024, 16384], P(('st', 'fq')), may hold values from -6 to 6
- freq_bins: int32 [1024], replicated, may hold values from 1 to 8191, as said below
- sensor_station: int32 [1024], P('st'), may hold values from 0 to 511, as said below
- gain: bfloat16 [1024, 768], P('st'), may hold values from -1.5 to 1.5
- damping: float32 [512, 768], P('st'), may hold values from 0 to 1
- damping_up: float32 [512, 768], P('st'), may hold values from 0 to 1
- phase_speed: float32 [768], replicated, may hold values from 0.5 to 4
Outputs:
- estimate: bfloat16 [512, 768, 1024], P(('st', 'fq'))
The draws below stay inside these ranges and needn't reach their ends.
Inputs may be any that keep to these rules, and one draw needn't show every extreme that they name: `freq_bins`: distinct bin numbers. `sensor_station`: sensor s sits at one of the 32 stations starting at (s // 64) * 32.
All inputs are finite; a program needn't handle non-finite values.
Results may differ from the reference program's by a relative error of at most 0.015.
Values may be sent and summed in bfloat16 or wider, within the bound.
No kernel may reach another device: no remote copies, remote signals or barrier semaphores. Data moves between devices by JAX's collectives and lax.ppermute only.
A program may use at most 256 MiB of HBM per device.

```python
import math
import jax
import jax.numpy as jnp
from jax import lax

NT = 16384
M = 768
NF = 1024
ST_DEV = 32
SENS_GRP = 64
TOUT = 1024
STATIONS = 512
SENS = 1024


def draw_freq_bins(key, part):
    order = jax.random.permutation(jax.random.fold_in(key, 11), NT // 2 - 1)
    return (order[:NF] + 1).astype(jnp.int32)


def draw_sensor_station(key, part):
    groups = jnp.arange(SENS, dtype=jnp.int32) // SENS_GRP
    offsets = jax.random.randint(jax.random.fold_in(key, 23), (SENS,), 0, ST_DEV, dtype=jnp.int32)
    return (groups * ST_DEV + offsets).astype(jnp.int32)


def decay_table(key):
    keys = jax.random.split(key, 7)
    share = 0.5
    fast = jax.random.uniform(keys[0], (M,)) < share
    fast_rate = jax.random.uniform(keys[1], (M,), minval=2.3 / (0.75 * ST_DEV), maxval=2.3 / (0.5 * ST_DEV))
    slow_rate = jax.random.uniform(keys[2], (M,), minval=0.1, maxval=0.5) * (2.3 / STATIONS)
    rate = jnp.where(fast, fast_rate, slow_rate)
    blocks = jnp.arange(STATIONS, dtype=jnp.int32) // ST_DEV
    block_factor = jnp.exp(jax.random.uniform(keys[3], (STATIONS // ST_DEV,), minval=-0.35, maxval=0.35))
    station_factor = jax.random.uniform(keys[4], (STATIONS, 1), minval=0.8, maxval=1.2)
    damping_coefficients = rate[None, :] * block_factor[blocks][:, None] * station_factor
    probe_positions = jax.random.randint(keys[5], (2,), 0, STATIONS, dtype=jnp.int32)
    boundary_distances = jax.random.uniform(keys[6], (2,), minval=0.55, maxval=0.8)
    measurement_planes = jnp.arange(STATIONS, dtype=jnp.int32)
    excitation_pulse = jnp.where(measurement_planes == probe_positions[0], boundary_distances[0], 1.0) * jnp.where(measurement_planes == probe_positions[1], boundary_distances[1], 1.0)
    return (jnp.exp(-damping_coefficients) * excitation_pulse[:, None]).astype(jnp.float32)


def draw_damping(key, part):
    return decay_table(jax.random.fold_in(key, 101))


def draw_damping_up(key, part):
    return decay_table(jax.random.fold_in(key, 202))


def shard_levels(rng, extent, pieces, smallest, top_value):
    level = 1.0
    for position, parts in pieces:
        heights = jax.random.uniform(jax.random.fold_in(jax.random.fold_in(rng, 6), position), (parts,), jnp.float32, smallest / len(pieces), top_value / len(pieces))
        level = level * jnp.repeat(jnp.exp(heights), extent[position] // parts).reshape((-1,) + (1,) * (len(extent) - 1 - position))
    return level


def centred(stream_key, extent, spread, most, cuts=(), kind=jnp.bfloat16):
    loudness = shard_levels(stream_key, extent, cuts, -0.22, 0.18) if cuts else 1.0
    entries = jax.random.normal(stream_key, extent, jnp.float32) * spread * loudness
    return jnp.minimum(jnp.maximum(entries, -most), most).astype(kind)


def setup_inputs(seed: int = 0) -> dict:
    key_of = jax.random.split(jax.random.key(seed), 8)
    signals = centred(key_of[0], (SENS, NT), 1.0, 6.0, ((0, 128),))
    freq_bins = draw_freq_bins(jax.random.fold_in(key_of[7], 71), 0)
    sensor_station = draw_sensor_station(jax.random.fold_in(key_of[7], 71), 0)
    gain = centred(key_of[3], (SENS, M), 16 ** -0.5, 1.5, ((0, 16),))
    damping = draw_damping(jax.random.fold_in(key_of[7], 71), 0)
    damping_up = draw_damping_up(jax.random.fold_in(key_of[7], 71), 0)
    phase_speed = jnp.clip(jnp.exp(jax.random.uniform(key_of[6], (M,), jnp.float32, math.log(0.5), math.log(4.0))), 0.5, 4.0)
    return {"signals": signals, "freq_bins": freq_bins, "sensor_station": sensor_station, "gain": gain, "damping": damping, "damping_up": damping_up, "phase_speed": phase_speed}


def cmul(left, right):
    return jnp.stack([left[0] * right[0] - left[1] * right[1], left[0] * right[1] + left[1] * right[0]])

def reference(signals, freq_bins, sensor_station, gain, damping, damping_up, phase_speed):
    n_blocks = STATIONS // ST_DEV
    times = lax.iota(jnp.int32, NT)
    hann = 0.5 - 0.5 * jnp.cos(times.astype(jnp.float32) * (2 * math.pi / NT))
    windowed = (signals.astype(jnp.float32) * hann[None, :]).astype(jnp.bfloat16)
    angle = (times[:, None] * freq_bins[None, :] % NT).astype(jnp.float32) * (2 * math.pi / NT)
    cos_table = (jnp.cos(angle) / math.sqrt(NT)).astype(jnp.bfloat16)
    sin_table = (jnp.sin(angle) / math.sqrt(NT)).astype(jnp.bfloat16)
    spec_re = jnp.dot(windowed, cos_table, preferred_element_type=jnp.float32).astype(jnp.bfloat16)
    spec_im = (-jnp.dot(windowed, sin_table, preferred_element_type=jnp.float32)).astype(jnp.bfloat16)
    theta = 2 * math.pi * (freq_bins.astype(jnp.float32) / NT)[:, None] * phase_speed[None, :]
    rot_down = jnp.stack([jnp.cos(theta), -jnp.sin(theta)])
    rot_up = jnp.stack([jnp.cos(theta), jnp.sin(theta)])
    spectra = jnp.stack([spec_re, spec_im]).astype(jnp.float32)
    gain_wide = gain.astype(jnp.float32)
    zeros = jnp.zeros((2, NF, M), jnp.float32)
    t_out = NT - TOUT + lax.iota(jnp.int32, TOUT)
    out_angle = (freq_bins[:, None] * t_out[None, :] % NT).astype(jnp.float32) * (2 * math.pi / NT)
    inverse = jnp.stack([jnp.cos(out_angle) / math.sqrt(NF), -jnp.sin(out_angle) / math.sqrt(NF)]).astype(jnp.bfloat16)

    def block_forcing(block):
        first = (block * SENS_GRP).astype(jnp.int32)
        spec_block = lax.dynamic_slice_in_dim(spectra, first, SENS_GRP, 1)
        gain_block = lax.dynamic_slice_in_dim(gain_wide, first, SENS_GRP, 0)
        local = lax.dynamic_slice_in_dim(sensor_station, first, SENS_GRP, 0) - block * ST_DEV
        outer = jnp.transpose(spec_block, (1, 0, 2))[:, :, :, None] * gain_block[:, None, None, :]
        return jnp.zeros((ST_DEV, 2, NF, M), jnp.float32).at[local].add(outer)

    def rows_of(table, block):
        return lax.dynamic_slice_in_dim(table, (block * ST_DEV).astype(jnp.int32), ST_DEV, 0)

    def down_step(state, inputs):
        term, rate = inputs
        state = cmul(rate[None, None, :] * rot_down, state) + term
        return (state, state)

    def up_step(state, inputs):
        term, rate = inputs
        state = cmul(rate[None, None, :] * rot_up, state) + term
        return (state, state)

    def first_pass(entering, block):
        forcing = block_forcing(block)
        leaving, unused = lax.scan(down_step, entering, (forcing, rows_of(damping, block)))
        return (leaving, entering)
    final_down, entering_all = lax.scan(first_pass, zeros, jnp.arange(n_blocks, dtype=jnp.int32))

    def second_pass(entering_up, inputs):
        block, entering_down = inputs
        forcing = block_forcing(block)
        leaving_up, upstream = lax.scan(up_step, entering_up, (forcing, rows_of(damping_up, block)), reverse=True)
        unused, downstream = lax.scan(down_step, entering_down, (forcing, rows_of(damping, block)))
        state = (downstream + upstream).astype(jnp.bfloat16)
        estimator_answer = jnp.einsum('kcfm,cft->kmt', state.astype(jnp.float32), inverse.astype(jnp.float32)).astype(jnp.bfloat16)
        return (leaving_up, estimator_answer)
    final_up, blocks_out = lax.scan(second_pass, zeros, (jnp.arange(n_blocks, dtype=jnp.int32), entering_all), reverse=True)
    return blocks_out.reshape(STATIONS, M, TOUT)
```

```python
import math

import jax
import jax.numpy as jnp
from jax import lax
from jax.experimental import pallas as pl
from jax.experimental.pallas import tpu as pltpu
from jax.sharding import Mesh
from jax.sharding import PartitionSpec as P

NT = 16384
TOUT = 1024
BLOCK = 32
GROUP = 8
OWN = 4
TILE = 128
SLICE = 48
ALL = ("st", "z", "core")
FQ = ("z", "core")
MIB = 1 << 20

COS = (1.0, -19.739208221435547, 64.93939208984375, -85.45665740966797, 60.242130279541016,
       -26.4046688079834, 7.800131797790527, -1.4531123638153076)
SIN = (6.2831854820251465, -41.34170150756836, 81.60513305664062, -76.70301818847656,
       42.02592849731445, -14.899847984313965, 3.238137722015381)


def horner(terms, y):
    total = y * terms[-1] + terms[-2]
    for term in terms[-3::-1]:
        total = total * y + term
    return total


def cos_sin(turns):
    r = turns - jnp.floor(turns + 0.5)
    y = r * r
    return horner(COS, y), r * horner(SIN, y)


def table_turns(steps, bins):
    return ((steps * bins) & (NT - 1)).astype(jnp.float32) * (1.0 / NT)


def spectrum_kernel(signals_ref, bins_ref, out_ref, windowed):
    sensors = out_ref.shape[1]
    coarse = lax.broadcasted_iota(jnp.int32, (128, 128), 0)
    fine = lax.broadcasted_iota(jnp.int32, (128, 128), 1)

    @pl.when(pl.program_id(0) == 0)
    def _():
        times = (coarse * 128 + fine).astype(jnp.float32)
        hann = 0.5 - 0.5 * cos_sin(times * (1.0 / NT))[0]
        for s in range(sensors):
            rows = pl.ds(s * 128, 128)
            windowed[rows, :] = (signals_ref[rows, :].astype(jnp.float32) * hann).astype(jnp.bfloat16)

    bins = bins_ref[0, 0:1, :]
    c1, s1 = cos_sin(table_turns(coarse, bins))
    table = jnp.concatenate(
        [(c1 * (1 / 128)).astype(jnp.bfloat16), (s1 * (-1 / 128)).astype(jnp.bfloat16)], axis=1
    )
    c2, s2 = cos_sin(table_turns(coarse * 128, bins))
    for s in range(sensors):
        part = jnp.dot(windowed[pl.ds(s * 128, 128), :], table, preferred_element_type=jnp.float32)
        re, im = part[:, :TILE], part[:, TILE:]
        out_ref[0, s:s + 1, :TILE] = jnp.sum(re * c2 + im * s2, axis=0, keepdims=True)
        out_ref[0, s:s + 1, TILE:] = jnp.sum(im * c2 - re * s2, axis=0, keepdims=True)


def spectrum(signals, freq_bins):
    sensors = signals.shape[0]
    tiles = freq_bins.shape[0] // TILE
    bins = jnp.broadcast_to(freq_bins.reshape(tiles, 1, TILE), (tiles, 8, TILE))
    return pl.pallas_call(
        spectrum_kernel,
        grid=(tiles,),
        in_specs=[
            pl.BlockSpec((sensors * 128, 128), lambda q: (0, 0)),
            pl.BlockSpec((1, 8, TILE), lambda q: (q, 0, 0)),
        ],
        out_specs=pl.BlockSpec((1, sensors, 2 * TILE), lambda q: (q, 0, 0)),
        out_shape=jax.ShapeDtypeStruct((tiles, sensors, 2 * TILE), jnp.float32),
        scratch_shapes=[pltpu.VMEM((sensors * 128, 128), jnp.bfloat16)],
        compiler_params=pltpu.CompilerParams(vmem_limit_bytes=24 * MIB),
        cost_estimate=pl.CostEstimate(flops=2 * 10**9, bytes_accessed=10**6, transcendentals=0),
        name="spectrum",
    )(signals.reshape(sensors * 128, 128), bins)


def inverse_kernel(bins_ref, out_ref):
    times = lax.broadcasted_iota(jnp.int32, (TILE, TOUT), 1) + (NT - TOUT)
    c, s = cos_sin(table_turns(times, bins_ref[:, 0:1]))
    out_ref[:TILE, :] = (c * (1 / 32)).astype(jnp.bfloat16)
    out_ref[TILE:, :] = (s * (-1 / 32)).astype(jnp.bfloat16)


def inverse_table(freq_bins):
    tiles = freq_bins.shape[0] // TILE
    bins = jnp.broadcast_to(freq_bins[:, None], (tiles * TILE, 128))
    return pl.pallas_call(
        inverse_kernel,
        grid=(tiles,),
        in_specs=[pl.BlockSpec((TILE, 128), lambda q: (q, 0))],
        out_specs=pl.BlockSpec((2 * TILE, TOUT), lambda q: (q, 0)),
        out_shape=jax.ShapeDtypeStruct((tiles * 2 * TILE, TOUT), jnp.bfloat16),
        compiler_params=pltpu.CompilerParams(vmem_limit_bytes=24 * MIB),
        cost_estimate=pl.CostEstimate(flops=4 * 10**9, bytes_accessed=5 * 10**6, transcendentals=0),
        name="inverse_table",
    )(bins)


def step(rate, c, s, re, im, f_re, f_im):
    return rate * (c * re - s * im) + f_re, rate * (c * im + s * re) + f_im


def march_kernel(tables_ref, spec_ref, rot_ref, out_ref, sel, force):
    blocks = tables_ref.shape[0]

    def forcing(block, slot):
        gain = tables_ref[block, :SLICE, :64]
        local = tables_ref[block, SLICE:SLICE + 1, :64]
        for k in range(BLOCK):
            sel[slot, pl.ds(k * SLICE, SLICE), :] = jnp.where(
                local == jnp.float32(k), gain, 0.0
            ).astype(jnp.bfloat16)
        force[slot] = jnp.dot(sel[slot], spec_ref[block], preferred_element_type=jnp.float32)

    def body(b, carry):
        d_re, d_im, u_re, u_im = carry
        up = blocks - 1 - b
        forcing(b, 0)
        forcing(up, 1)
        c, s = rot_ref[0], rot_ref[1]
        down_rates = tables_ref[b, :SLICE, :]
        up_rates = tables_ref[up, :SLICE, :]
        for k in range(BLOCK):
            if k % GROUP == 0:
                group = 2 * (b * (BLOCK // GROUP) + k // GROUP)
                out_ref[group, :SLICE, :] = d_re.astype(jnp.bfloat16)
                out_ref[group, SLICE:, :] = d_im.astype(jnp.bfloat16)
            rows = pl.ds(k * SLICE, SLICE)
            d_re, d_im = step(
                down_rates[:, 64 + k:65 + k], c, -s, d_re, d_im,
                force[0, rows, :TILE], force[0, rows, TILE:],
            )
            j = BLOCK - 1 - k
            if j % GROUP == GROUP - 1:
                group = 2 * (up * (BLOCK // GROUP) + j // GROUP) + 1
                out_ref[group, :SLICE, :] = u_re.astype(jnp.bfloat16)
                out_ref[group, SLICE:, :] = u_im.astype(jnp.bfloat16)
            rows = pl.ds(j * SLICE, SLICE)
            u_re, u_im = step(
                up_rates[:, 96 + j:97 + j], c, s, u_re, u_im,
                force[1, rows, :TILE], force[1, rows, TILE:],
            )
        return d_re, d_im, u_re, u_im

    zero = jnp.zeros((SLICE, TILE), jnp.float32)
    lax.fori_loop(0, blocks, body, (zero, zero, zero, zero))


def entering_states(tables, spec, rot):
    blocks = tables.shape[0]
    return pl.pallas_call(
        march_kernel,
        out_shape=jax.ShapeDtypeStruct(
            (2 * blocks * BLOCK // GROUP, 2 * SLICE, TILE), jnp.bfloat16
        ),
        in_specs=[pl.BlockSpec(memory_space=pltpu.VMEM)] * 3,
        out_specs=pl.BlockSpec(memory_space=pltpu.VMEM),
        scratch_shapes=[
            pltpu.VMEM((2, BLOCK * SLICE, 64), jnp.bfloat16),
            pltpu.VMEM((2, BLOCK * SLICE, 2 * TILE), jnp.float32),
        ],
        compiler_params=pltpu.CompilerParams(vmem_limit_bytes=24 * MIB),
        cost_estimate=pl.CostEstimate(flops=20 * 10**9, bytes_accessed=5 * 10**6, transcendentals=0),
        name="entering_states",
    )(tables, spec, rot)


def estimate_kernel(
    core_ref, near_ref, far_ref, gain_ref, rates_ref, spec_ref, omega_ref, inverse_ref,
    out_ref, state, force, kept,
):
    slices = near_ref.shape[0]
    tiles = near_ref.shape[1]
    core = core_ref[0]

    def fill(q, unused):
        lane = pl.multiple_of(q * 2 * TILE, 2 * TILE)
        omega = omega_ref[q, 0:1, :]
        for t in range(slices):
            force[...] = jnp.dot(gain_ref[t], spec_ref[q], preferred_element_type=jnp.float32)
            rates = rates_ref[t]
            c, s = cos_sin(omega * rates[:, GROUP + OWN:GROUP + OWN + 1])
            re = near_ref[t, q, :SLICE, :].astype(jnp.float32)
            im = near_ref[t, q, SLICE:, :].astype(jnp.float32)
            for i in range(OWN):
                rows = pl.ds((GROUP - 1 - i) * SLICE, SLICE)
                re, im = step(
                    rates[:, GROUP + i:GROUP + i + 1], c, -s, re, im,
                    force[rows, :TILE], force[rows, TILE:],
                )
                kept[i, 0], kept[i, 1] = re, im
            re = far_ref[t, q, :SLICE, :].astype(jnp.float32)
            im = far_ref[t, q, SLICE:, :].astype(jnp.float32)
            for i in range(GROUP):
                rows = pl.ds(i * SLICE, SLICE)
                re, im = step(
                    rates[:, i:i + 1], c, s, re, im, force[rows, :TILE], force[rows, TILE:]
                )
                if i >= GROUP - OWN:
                    n = GROUP - 1 - i
                    own = jnp.where(core == 0, n, OWN - 1 - n)
                    rows = pl.ds(t * SLICE, SLICE)
                    state[own, rows, pl.ds(lane, TILE)] = (re + kept[n, 0]).astype(jnp.bfloat16)
                    state[own, rows, pl.ds(lane + TILE, TILE)] = (im + kept[n, 1]).astype(jnp.bfloat16)
        return unused

    lax.fori_loop(0, tiles, fill, 0)
    height = slices * SLICE

    def multiply(n, unused):
        columns = pl.ds(pl.multiple_of(n * 256, 256), 256)
        out = jnp.dot(
            state[...].reshape(OWN * height, 2 * tiles * TILE), inverse_ref[:, columns],
            preferred_element_type=jnp.float32,
        )
        out_ref[:, :, columns] = out.astype(jnp.bfloat16).reshape(OWN, height, 256)
        return unused

    lax.fori_loop(0, TOUT // 256, multiply, 0)


def estimates(core, near, far, gain, rates, spec, omega, inverse):
    slices, tiles = near.shape[:2]
    per = 4
    once = pl.Buffered(1)
    whole = lambda a: pl.BlockSpec(a.shape, lambda i: (0,) * a.ndim, pipeline_mode=once)
    return pl.pallas_call(
        estimate_kernel,
        grid=(slices // per,),
        in_specs=[
            pl.BlockSpec(memory_space=pltpu.SMEM),
            pl.BlockSpec((per, tiles, 2 * SLICE, TILE), lambda i: (i, 0, 0, 0)),
            pl.BlockSpec((per, tiles, 2 * SLICE, TILE), lambda i: (i, 0, 0, 0)),
            pl.BlockSpec((per, GROUP * SLICE, 64), lambda i: (i, 0, 0)),
            pl.BlockSpec((per, SLICE, 128), lambda i: (i, 0, 0)),
            whole(spec),
            whole(omega),
            whole(inverse),
        ],
        out_specs=pl.BlockSpec((OWN, per * SLICE, TOUT), lambda i: (0, i, 0)),
        out_shape=jax.ShapeDtypeStruct((OWN, slices * SLICE, TOUT), jnp.bfloat16),
        scratch_shapes=[
            pltpu.VMEM((OWN, per * SLICE, 2 * tiles * TILE), jnp.bfloat16),
            pltpu.VMEM((GROUP * SLICE, 2 * TILE), jnp.float32),
            pltpu.VMEM((OWN, 2, SLICE, TILE), jnp.float32),
        ],
        compiler_params=pltpu.CompilerParams(vmem_limit_bytes=40 * MIB),
        cost_estimate=pl.CostEstimate(flops=40 * 10**9, bytes_accessed=20 * 10**6, transcendentals=0),
        name="estimates",
    )(core, near, far, gain, rates, spec, omega, inverse)


def on_device(signals, freq_bins, sensor_station, gain, damping, damping_up, phase_speed):
    st, z, core = (lax.axis_index(axis) for axis in ALL)
    blocks = lax.axis_size("st")
    tiles = freq_bins.shape[0] // TILE
    sensors = sensor_station.shape[0]
    local = sensor_station - st * BLOCK
    wide_gain = gain.astype(jnp.float32)

    columns = jnp.concatenate([wide_gain, damping, damping_up], axis=0)
    columns = columns.T.reshape(blocks, SLICE, sensors + 2 * BLOCK)
    places = jnp.pad(local.astype(jnp.float32), (0, 2 * BLOCK))
    places = jnp.broadcast_to(places, (blocks, 8, sensors + 2 * BLOCK))
    tables = lax.all_to_all(
        jnp.concatenate([columns, places], axis=1), "st", split_axis=0, concat_axis=0, tiled=True
    )

    spec = spectrum(signals, freq_bins).astype(jnp.bfloat16)
    to_all = jnp.broadcast_to(spec[None], (blocks,) + spec.shape).reshape((-1,) + spec.shape[1:])
    spec_tile = lax.all_to_all(to_all, ALL, split_axis=0, concat_axis=0, tiled=True)
    spec_tile = spec_tile.reshape(blocks, sensors, 2 * TILE)
    to_fq = jnp.broadcast_to(spec[None], (tiles,) + spec.shape)
    spec_block = lax.all_to_all(to_fq, FQ, split_axis=0, concat_axis=0, tiled=True)
    spec_block = spec_block.transpose(1, 0, 2, 3).reshape(tiles, sensors, 2 * TILE)

    omega = (freq_bins.astype(jnp.float32) / NT).reshape(tiles, 1, TILE)
    own_omega = lax.dynamic_index_in_dim(omega, z * 2 + core, 0, keepdims=False)
    own_speed = lax.dynamic_slice_in_dim(phase_speed, st * SLICE, SLICE)
    theta = 2 * math.pi * own_omega * own_speed[:, None]
    rot = jnp.stack([jnp.cos(theta), jnp.sin(theta)])
    entering = entering_states(tables, spec_tile, rot)

    near = lax.all_to_all(entering, ALL, split_axis=0, concat_axis=0, tiled=True)
    far = lax.ppermute(near, "core", [(0, 1), (1, 0)])
    shape = (blocks, tiles, 2 * SLICE, TILE)

    first = z * GROUP
    eight = lax.iota(jnp.int32, GROUP)
    far_order = first + jnp.where(core == 0, GROUP - 1 - eight, eight)
    near_order = far_order[:GROUP - OWN - 1:-1]
    far_rates = jnp.where(core == 0, damping_up[far_order], damping[far_order])
    near_rates = jnp.where(core == 0, damping[near_order], damping_up[near_order])
    turn = jnp.where(core == 0, phase_speed, -phase_speed)[None]
    rates = jnp.concatenate([far_rates, near_rates, turn], axis=0)
    rates = jnp.pad(rates, ((0, 128 - rates.shape[0]), (0, 0))).T.reshape(blocks, SLICE, 128)
    slices_gain = gain.T.reshape(blocks, 1, SLICE, sensors)
    at = (local[None, :] == far_order[:, None])[None, :, None, :]
    own_gain = jnp.where(at, slices_gain, 0).reshape(blocks, GROUP * SLICE, sensors)

    return estimates(
        core.reshape(1).astype(jnp.int32),
        near.reshape(shape),
        far.reshape(shape),
        own_gain,
        rates,
        spec_block,
        jnp.broadcast_to(omega, (tiles, 8, TILE)),
        inverse_table(freq_bins),
    )


def solution(mesh):
    torus = Mesh(mesh.devices.reshape(mesh.shape["st"], 4, 2), ALL)
    placed = (P(ALL, None), P(), P("st"), P("st", None), P("st", None), P("st", None), P())
    return jax.shard_map(
        on_device, mesh=torus, in_specs=placed, out_specs=P(ALL, None, None), check_vma=False
    )
```

```python
import math

import jax
import jax.numpy as jnp
from jax import lax
from jax.experimental import pallas as pl
from jax.experimental.pallas import tpu as pltpu
from jax.sharding import Mesh
from jax.sharding import PartitionSpec as P

NT = 16384
TOUT = 1024
BLOCK = 32
GROUP = 8
OWN = 4
TILE = 128
SLICE = 48
ALL = ("st", "z", "core")
FQ = ("z", "core")
MIB = 1 << 20

COS = (1.0, -19.739208221435547, 64.93939208984375, -85.45665740966797, 60.242130279541016,
       -26.4046688079834, 7.800131797790527, -1.4531123638153076)
SIN = (6.2831854820251465, -41.34170150756836, 81.60513305664062, -76.70301818847656,
       42.02592849731445, -14.899847984313965, 3.238137722015381)


def horner(terms, y):
    total = y * terms[-1] + terms[-2]
    for term in terms[-3::-1]:
        total = total * y + term
    return total


def cos_sin(turns):
    r = turns - jnp.floor(turns + 0.5)
    y = r * r
    return horner(COS, y), r * horner(SIN, y)


def table_turns(steps, bins):
    return ((steps * bins) & (NT - 1)).astype(jnp.float32) * (1.0 / NT)


def spectrum_kernel(
    fq_ref, signals_ref, bins_ref, gain_ref, damping_ref, damping_up_ref, places_ref,
    send_ref, spec_ref, windowed, tables,
):
    sensors = spec_ref.shape[1]
    slices = send_ref.shape[0]
    q = pl.program_id(0)
    coarse = lax.broadcasted_iota(jnp.int32, (128, 128), 0)
    fine = lax.broadcasted_iota(jnp.int32, (128, 128), 1)

    @pl.when(q == 0)
    def _():
        times = (coarse * 128 + fine).astype(jnp.float32)
        hann = 0.5 - 0.5 * cos_sin(times * (1.0 / NT))[0]
        for s in range(sensors):
            rows = pl.ds(s * 128, 128)
            windowed[rows, :] = (signals_ref[rows, :].astype(jnp.float32) * hann).astype(jnp.bfloat16)
        values = jnp.concatenate(
            [gain_ref[...].astype(jnp.float32), damping_ref[...], damping_up_ref[...]], axis=0
        ).T
        high = values.astype(jnp.bfloat16).astype(jnp.float32)
        rest = values - high
        middle = rest.astype(jnp.bfloat16).astype(jnp.float32)
        low = rest - middle
        tables[:, :SLICE, :128] = high.reshape(slices, SLICE, 128)
        tables[:, :SLICE, 128:] = (middle + pltpu.roll(low, 64, 1)).reshape(slices, SLICE, 128)
        tables[:, SLICE:, :] = jnp.zeros((slices, 64 - SLICE, 256), jnp.float32)
        for n in range(slices):
            tables[n, SLICE:SLICE + 8, :128] = places_ref[...]

    bins = bins_ref[pl.ds(q, 1), :]
    c1, s1 = cos_sin(table_turns(coarse, bins))
    table = jnp.concatenate(
        [(c1 * (1 / 128)).astype(jnp.bfloat16), (s1 * (-1 / 128)).astype(jnp.bfloat16)], axis=1
    )
    c2, s2 = cos_sin(table_turns(coarse * 128, bins))
    for s in range(sensors):
        part = jnp.dot(windowed[pl.ds(s * 128, 128), :], table, preferred_element_type=jnp.float32)
        re, im = part[:, :TILE], part[:, TILE:]
        spec_ref[0, s:s + 1, :TILE] = jnp.sum(re * c2 + im * s2, axis=0, keepdims=True)
        spec_ref[0, s:s + 1, TILE:] = jnp.sum(im * c2 - re * s2, axis=0, keepdims=True)
    own = spec_ref[0]
    rows = pl.ds(pl.multiple_of(fq_ref[0] * 8, 8), 8)
    for n in range(slices):
        send_ref[n, 0] = jnp.concatenate([own, tables[n, rows, :]], axis=0).astype(jnp.bfloat16)


def spectrum(fq, signals, freq_bins, gain, damping, damping_up, places, slices):
    sensors = signals.shape[0]
    tiles = freq_bins.shape[0] // TILE
    bins = freq_bins.reshape(tiles, TILE)
    whole = lambda a: pl.BlockSpec(a.shape, lambda q: (0, 0))
    signals = signals.reshape(sensors * 128, 128)
    return pl.pallas_call(
        spectrum_kernel,
        grid=(tiles,),
        in_specs=[
            pl.BlockSpec(memory_space=pltpu.SMEM),
            whole(signals),
            whole(bins),
            whole(gain),
            whole(damping),
            whole(damping_up),
            whole(places),
        ],
        out_specs=[
            pl.BlockSpec((slices, 1, 16, 2 * TILE), lambda q: (0, q, 0, 0)),
            pl.BlockSpec((1, sensors, 2 * TILE), lambda q: (q, 0, 0)),
        ],
        out_shape=[
            jax.ShapeDtypeStruct((slices, tiles, 16, 2 * TILE), jnp.bfloat16),
            jax.ShapeDtypeStruct((tiles, sensors, 2 * TILE), jnp.float32),
        ],
        scratch_shapes=[
            pltpu.VMEM((sensors * 128, 128), jnp.bfloat16),
            pltpu.VMEM((slices, 64, 2 * TILE), jnp.float32),
        ],
        compiler_params=pltpu.CompilerParams(vmem_limit_bytes=56 * MIB),
        cost_estimate=pl.CostEstimate(flops=2 * 10**9, bytes_accessed=10**6, transcendentals=0),
        name="spectrum",
    )(fq, signals, bins, gain, damping, damping_up, places)


def inverse_kernel(bins_ref, after_ref, out_ref):
    del after_ref
    bins = bins_ref[:, 0:1]
    lane = lax.broadcasted_iota(jnp.int32, (TILE, 128), 1)
    c1, s1 = cos_sin(table_turns(lane, bins))
    c2, s2 = cos_sin(table_turns(lane * 128 + (NT - TOUT), bins))
    c2, s2 = c2 * (1 / 32), s2 * (1 / 32)
    for n in range(TOUT // 128):
        c, s = c2[:, n:n + 1], s2[:, n:n + 1]
        columns = pl.ds(n * 128, 128)
        out_ref[:TILE, columns] = (c1 * c - s1 * s).astype(jnp.bfloat16)
        out_ref[TILE:, columns] = (-s1 * c - c1 * s).astype(jnp.bfloat16)


def inverse_table(freq_bins, after):
    tiles = freq_bins.shape[0] // TILE
    bins = jnp.broadcast_to(freq_bins[:, None], (tiles * TILE, 128))
    return pl.pallas_call(
        inverse_kernel,
        grid=(tiles,),
        in_specs=[
            pl.BlockSpec((TILE, 128), lambda q: (q, 0)),
            pl.BlockSpec(memory_space=pl.ANY),
        ],
        out_specs=pl.BlockSpec((2 * TILE, TOUT), lambda q: (q, 0)),
        out_shape=jax.ShapeDtypeStruct((tiles * 2 * TILE, TOUT), jnp.bfloat16),
        compiler_params=pltpu.CompilerParams(vmem_limit_bytes=56 * MIB),
        cost_estimate=pl.CostEstimate(flops=4 * 10**9, bytes_accessed=5 * 10**6, transcendentals=0),
        name="inverse_table",
    )(bins, after)


def turn(c, s, re, im):
    return c * re - s * im, c * im + s * re


def turn_back(c, s, re, im):
    return c * re + s * im, c * im - s * re


def step(rate, turned, f_re, f_im):
    return rate * turned[0] + f_re, rate * turned[1] + f_im


def march_kernel(recv_ref, rot_ref, out_ref, done_ref, force):
    done_ref[...] = jnp.zeros_like(done_ref)
    tiles = 8
    blocks = recv_ref.shape[0] // tiles

    def table_rows(block, p):
        return recv_ref[block * tiles + p].astype(jnp.float32)[8:]

    def forcing(block, stations, slot):
        gain = jnp.concatenate([table_rows(block, p) for p in range(SLICE // 8)], axis=0)[:, :64]
        local = table_rows(block, SLICE // 8)[0:1, :64]
        spec = jnp.concatenate(
            [recv_ref[block * tiles + p].astype(jnp.float32)[:8] for p in range(tiles)], axis=0
        ).astype(jnp.bfloat16)
        chosen = jnp.concatenate(
            [jnp.where(local == jnp.float32(k), gain, 0.0) for k in stations], axis=0
        ).astype(jnp.bfloat16)
        slot[...] = jnp.dot(chosen, spec, preferred_element_type=jnp.float32)

    def rates_of(block):
        both = jnp.concatenate([table_rows(block, p) for p in range(SLICE // 8)], axis=0)
        rest = both[:, 128:]
        return both[:, :128] + rest + pltpu.roll(rest, 64, 1)

    chunks = BLOCK // GROUP
    down_of = [range(n * GROUP, n * GROUP + GROUP) for n in range(chunks)]
    up_of = [range(BLOCK - 1 - n * GROUP, BLOCK - 1 - n * GROUP - GROUP, -1) for n in range(chunks)]

    def body(b, carry):
        d_re, d_im, u_re, u_im = carry
        up = blocks - 1 - b
        c, s = rot_ref[0], rot_ref[1]
        down_rates = rates_of(b)
        up_rates = rates_of(up)
        for n in range(chunks):
            now, later = n % 2, (n + 1) % 2
            if n + 1 < chunks:
                forcing(b, down_of[n + 1], force.at[later, 0])
                forcing(up, up_of[n + 1], force.at[later, 1])
            else:
                forcing(jnp.minimum(b + 1, blocks - 1), down_of[0], force.at[later, 0])
                forcing(jnp.maximum(up - 1, 0), up_of[0], force.at[later, 1])
            group = 2 * (b * chunks + n)
            out_ref[group, :SLICE, :] = d_re.astype(jnp.bfloat16)
            out_ref[group, SLICE:, :] = d_im.astype(jnp.bfloat16)
            group = 2 * (up * chunks + chunks - 1 - n) + 1
            out_ref[group, :SLICE, :] = u_re.astype(jnp.bfloat16)
            out_ref[group, SLICE:, :] = u_im.astype(jnp.bfloat16)
            for i in range(GROUP):
                rows = pl.ds(i * SLICE, SLICE)
                k, j = down_of[n][i], up_of[n][i]
                d_re, d_im = step(
                    down_rates[:, 64 + k:65 + k], turn_back(c, s, d_re, d_im),
                    force[now, 0, rows, :TILE], force[now, 0, rows, TILE:],
                )
                u_re, u_im = step(
                    up_rates[:, 96 + j:97 + j], turn(c, s, u_re, u_im),
                    force[now, 1, rows, :TILE], force[now, 1, rows, TILE:],
                )
        return d_re, d_im, u_re, u_im

    forcing(0, down_of[0], force.at[0, 0])
    forcing(blocks - 1, up_of[0], force.at[0, 1])
    zero = jnp.zeros((SLICE, TILE), jnp.float32)
    lax.fori_loop(0, blocks, body, (zero, zero, zero, zero))


def entering_states(recv, rot, blocks):
    return pl.pallas_call(
        march_kernel,
        out_shape=[
            jax.ShapeDtypeStruct((2 * blocks * BLOCK // GROUP, 2 * SLICE, TILE), jnp.bfloat16),
            jax.ShapeDtypeStruct((8, 128), jnp.float32),
        ],
        in_specs=[pl.BlockSpec(memory_space=pltpu.VMEM)] * 2,
        out_specs=[pl.BlockSpec(memory_space=pltpu.VMEM)] * 2,
        scratch_shapes=[pltpu.VMEM((2, 2, GROUP * SLICE, 2 * TILE), jnp.float32)],
        compiler_params=pltpu.CompilerParams(vmem_limit_bytes=56 * MIB),
        cost_estimate=pl.CostEstimate(flops=12 * 10**9, bytes_accessed=5 * 10**6, transcendentals=0),
        name="entering_states",
    )(recv, rot)


TURN = GROUP + OWN
SKIP = TURN + 1


def local_kernel(gain_ref, rates_ref, spec_ref, omega_ref, after_ref, part_ref, rot_ref, force, kept):
    del after_ref
    pair = force.shape[0]
    rates = rates_ref[0]

    def two(n, unused):
        for p in range(pair):
            q = n * pair + p
            force[p] = jnp.dot(gain_ref[0], spec_ref[q], preferred_element_type=jnp.float32)
        for p in range(pair):
            q = n * pair + p

            def forced(i):
                rows = pl.ds(i * SLICE, SLICE)
                return force[p, rows, :TILE], force[p, rows, TILE:]

            c, s = cos_sin(omega_ref[q, 0:1, :] * rates[:, TURN:TURN + 1])
            rot_ref[0, q, :SLICE, :] = c
            rot_ref[0, q, SLICE:, :] = s
            re, im = forced(GROUP - 1)
            kept[p, 0, 0], kept[p, 0, 1] = re, im
            for i in range(1, OWN):
                re, im = step(
                    rates[:, GROUP + i:GROUP + i + 1], turn_back(c, s, re, im),
                    *forced(GROUP - 1 - i),
                )
                kept[p, i, 0], kept[p, i, 1] = re, im
            re, im = forced(0)
            for i in range(1, GROUP):
                re, im = step(rates[:, i:i + 1], turn(c, s, re, im), *forced(i))
                if i >= GROUP - OWN:
                    n_own, n_near = i - (GROUP - OWN), GROUP - 1 - i
                    part_ref[0, q, n_own, :SLICE, :] = (re + kept[p, n_near, 0]).astype(jnp.bfloat16)
                    part_ref[0, q, n_own, SLICE:, :] = (im + kept[p, n_near, 1]).astype(jnp.bfloat16)
        return unused

    lax.fori_loop(0, spec_ref.shape[0] // pair, two, 0)


def local_states(gain, rates, spec, omega, after):
    slices, tiles = gain.shape[0], spec.shape[0]
    whole = lambda a: pl.BlockSpec(a.shape, lambda t: (0,) * a.ndim)
    return pl.pallas_call(
        local_kernel,
        grid=(slices,),
        in_specs=[
            pl.BlockSpec((1, GROUP * SLICE, 64), lambda t: (t, 0, 0)),
            pl.BlockSpec((1, SLICE, 128), lambda t: (t, 0, 0)),
            whole(spec),
            whole(omega),
            pl.BlockSpec(memory_space=pl.ANY),
        ],
        out_specs=[
            pl.BlockSpec((1, tiles, OWN, 2 * SLICE, TILE), lambda t: (t, 0, 0, 0, 0)),
            pl.BlockSpec((1, tiles, 2 * SLICE, TILE), lambda t: (t, 0, 0, 0)),
        ],
        out_shape=[
            jax.ShapeDtypeStruct((slices, tiles, OWN, 2 * SLICE, TILE), jnp.bfloat16),
            jax.ShapeDtypeStruct((slices, tiles, 2 * SLICE, TILE), jnp.float32),
        ],
        scratch_shapes=[
            pltpu.VMEM((2, GROUP * SLICE, 2 * TILE), jnp.float32),
            pltpu.VMEM((2, OWN, 2, SLICE, TILE), jnp.float32),
        ],
        compiler_params=pltpu.CompilerParams(vmem_limit_bytes=56 * MIB),
        cost_estimate=pl.CostEstimate(flops=20 * 10**9, bytes_accessed=20 * 10**6, transcendentals=0),
        name="local_states",
    )(gain, rates, spec, omega, after)


def estimate_kernel(
    core_ref, near_ref, far_ref, part_ref, rot_ref, rates_ref, inverse_ref, out_ref, even, odd, kept
):
    per, tiles = near_ref.shape[:2]
    height = per * SLICE
    index, last = pl.program_id(0), pl.num_programs(0) - 1
    core = core_ref[0]
    pieces = TOUT // 256

    def fill(state, q):
        lane = pl.multiple_of(q * 2 * TILE, 2 * TILE)
        for t in range(per):
            rates = rates_ref[t]
            c, s = rot_ref[t, q, :SLICE, :], rot_ref[t, q, SLICE:, :]
            re = near_ref[t, q, :SLICE, :].astype(jnp.float32)
            im = near_ref[t, q, SLICE:, :].astype(jnp.float32)
            for i in range(OWN):
                rate = rates[:, GROUP + i:GROUP + i + 1]
                re, im = turn_back(c, s, re, im)
                re, im = rate * re, rate * im
                kept[t, i, 0], kept[t, i, 1] = re, im
            c4, s4 = turn(c, s, c, s)
            c4, s4 = turn(c4, s4, c4, s4)
            re = far_ref[t, q, :SLICE, :].astype(jnp.float32)
            im = far_ref[t, q, SLICE:, :].astype(jnp.float32)
            re, im = turn(c4, s4, re, im)
            skip = rates[:, SKIP:SKIP + 1]
            re, im = skip * re, skip * im
            for i in range(OWN):
                rate = rates[:, GROUP - OWN + i:GROUP - OWN + i + 1]
                re, im = turn(c, s, re, im)
                re, im = rate * re, rate * im
                n = OWN - 1 - i
                own = jnp.where(core == 0, n, i)
                rows = pl.ds(t * SLICE, SLICE)
                whole_re = re + kept[t, n, 0] + part_ref[t, q, i, :SLICE, :].astype(jnp.float32)
                whole_im = im + kept[t, n, 1] + part_ref[t, q, i, SLICE:, :].astype(jnp.float32)
                state[own, rows, pl.ds(lane, TILE)] = whole_re.astype(jnp.bfloat16)
                state[own, rows, pl.ds(lane + TILE, TILE)] = whole_im.astype(jnp.bfloat16)

    def multiply(state, n):
        columns = pl.ds(pl.multiple_of(n * 256, 256), 256)
        out = jnp.dot(
            state[...].reshape(OWN * height, 2 * tiles * TILE), inverse_ref[:, columns],
            preferred_element_type=jnp.float32,
        )
        out_ref[:, :, columns] = out.astype(jnp.bfloat16).reshape(OWN, height, 256)

    def both(filled, multiplied):
        def piece(n, unused):
            if multiplied is not None:
                multiply(multiplied, n)
            if filled is not None:
                for p in range(tiles // pieces):
                    fill(filled, n * (tiles // pieces) + p)
            return unused

        lax.fori_loop(0, pieces, piece, 0)

    inner = (index > 0) & (index < last)
    pl.when(index == 0)(lambda: both(even, None))
    pl.when(inner & (index % 2 == 1))(lambda: both(odd, even))
    pl.when(inner & (index % 2 == 0))(lambda: both(even, odd))
    pl.when(index == last)(lambda: both(None, odd))


def estimates(core, near, far, part, rot, rates, inverse):
    slices, tiles = near.shape[:2]
    per = 4
    steps = slices // per
    assert steps % 2 == 0
    here = lambda i: jnp.minimum(i, steps - 1)
    return pl.pallas_call(
        estimate_kernel,
        grid=(steps + 1,),
        in_specs=[
            pl.BlockSpec(memory_space=pltpu.SMEM),
            pl.BlockSpec((per, tiles, 2 * SLICE, TILE), lambda i: (here(i), 0, 0, 0)),
            pl.BlockSpec((per, tiles, 2 * SLICE, TILE), lambda i: (here(i), 0, 0, 0)),
            pl.BlockSpec((per, tiles, OWN, 2 * SLICE, TILE), lambda i: (here(i), 0, 0, 0, 0)),
            pl.BlockSpec((per, tiles, 2 * SLICE, TILE), lambda i: (here(i), 0, 0, 0)),
            pl.BlockSpec((per, SLICE, 128), lambda i: (here(i), 0, 0)),
            pl.BlockSpec(inverse.shape, lambda i: (0, 0), pipeline_mode=pl.Buffered(1)),
        ],
        out_specs=pl.BlockSpec((OWN, per * SLICE, TOUT), lambda i: (0, jnp.maximum(i - 1, 0), 0)),
        out_shape=jax.ShapeDtypeStruct((OWN, slices * SLICE, TOUT), jnp.bfloat16),
        scratch_shapes=[
            pltpu.VMEM((OWN, per * SLICE, 2 * tiles * TILE), jnp.bfloat16),
            pltpu.VMEM((OWN, per * SLICE, 2 * tiles * TILE), jnp.bfloat16),
            pltpu.VMEM((per, OWN, 2, SLICE, TILE), jnp.float32),
        ],
        compiler_params=pltpu.CompilerParams(vmem_limit_bytes=40 * MIB),
        cost_estimate=pl.CostEstimate(flops=20 * 10**9, bytes_accessed=40 * 10**6, transcendentals=0),
        name="estimates",
    )(core, near, far, part, rot, rates, inverse)


def on_device(signals, freq_bins, sensor_station, gain, damping, damping_up, phase_speed):
    st, z, core = (lax.axis_index(axis) for axis in ALL)
    blocks = lax.axis_size("st")
    tiles = freq_bins.shape[0] // TILE
    sensors = sensor_station.shape[0]
    local = sensor_station - st * BLOCK
    places = jnp.broadcast_to(jnp.pad(local.astype(jnp.float32), (0, 128 - sensors)), (8, 128))

    fq = (z * 2 + core).astype(jnp.int32)
    send, spec = spectrum(fq.reshape(1), signals, freq_bins, gain, damping, damping_up, places, blocks)
    send = send.reshape((blocks * tiles,) + send.shape[2:])
    recv = lax.all_to_all(send, ALL, split_axis=0, concat_axis=0, tiled=True)
    to_fq = jnp.broadcast_to(spec.astype(jnp.bfloat16)[None], (tiles,) + spec.shape)
    spec_block = lax.all_to_all(to_fq, FQ, split_axis=0, concat_axis=0, tiled=True)
    spec_block = spec_block.transpose(1, 0, 2, 3).reshape(tiles, sensors, 2 * TILE)

    omega = (freq_bins.astype(jnp.float32) / NT).reshape(tiles, 1, TILE)
    own_omega = lax.dynamic_index_in_dim(omega, fq, 0, keepdims=False)
    own_speed = lax.dynamic_slice_in_dim(phase_speed, st * SLICE, SLICE)
    theta = 2 * math.pi * own_omega * own_speed[:, None]
    rot = jnp.stack([jnp.cos(theta), jnp.sin(theta)])
    entering, done = entering_states(recv, rot, blocks)
    near = lax.all_to_all(entering, ALL, split_axis=0, concat_axis=0, tiled=True)

    first = z * GROUP
    down = lax.dynamic_slice_in_dim(damping, first, GROUP)
    up = lax.dynamic_slice_in_dim(damping_up, first, GROUP)[::-1]
    far_rates = jnp.where(core == 0, up, down)
    near_rates = jnp.where(core == 0, down, up)[:OWN]
    speed = jnp.where(core == 0, phase_speed, -phase_speed)[None]
    skip = jnp.prod(far_rates[:GROUP - OWN], axis=0, keepdims=True)
    rates = jnp.concatenate([far_rates, near_rates, speed, skip], axis=0)
    rates = jnp.pad(rates, ((0, 128 - rates.shape[0]), (0, 0))).T.reshape(blocks, SLICE, 128)
    eight = lax.iota(jnp.int32, GROUP)
    far_order = first + jnp.where(core == 0, GROUP - 1 - eight, eight)
    at = (local[None, :] == far_order[:, None])[None, :, None, :]
    own_gain = jnp.where(at, gain.T.reshape(blocks, 1, SLICE, sensors), 0)
    own_gain = own_gain.reshape(blocks, GROUP * SLICE, sensors)

    part, turns = local_states(
        own_gain, rates, spec_block, jnp.broadcast_to(omega, (tiles, 8, TILE)), done
    )
    inverse = inverse_table(freq_bins, done)
    near, part, turns, inverse = lax.optimization_barrier((near, part, turns, inverse))
    far = lax.ppermute(near, "core", [(0, 1), (1, 0)])
    shape = (blocks, tiles, 2 * SLICE, TILE)
    return estimates(
        core.reshape(1).astype(jnp.int32), near.reshape(shape), far.reshape(shape), part, turns,
        rates, inverse,
    )


def solution(mesh):
    torus = Mesh(mesh.devices.reshape(mesh.shape["st"], 4, 2), ALL)
    placed = (P(ALL, None), P(), P("st"), P("st", None), P("st", None), P("st", None), P())
    return jax.shard_map(
        on_device, mesh=torus, in_specs=placed, out_specs=P(ALL, None, None), check_vma=False
    )
```

```python
import functools
import math

import jax
import jax.numpy as jnp
from jax import lax
from jax.experimental import pallas as pl
from jax.experimental.pallas import tpu as pltpu
from jax.sharding import Mesh
from jax.sharding import PartitionSpec as P

NT = 16384
TOUT = 1024
BLOCK = 32
GROUP = 8
OWN = 4
TILE = 128
SLICE = 48
ALL = ("st", "z", "core")
FQ = ("z", "core")
MIB = 1 << 20

COS = (1.0, -19.739208221435547, 64.93939208984375, -85.45665740966797, 60.242130279541016,
       -26.4046688079834, 7.800131797790527, -1.4531123638153076)
SIN = (6.2831854820251465, -41.34170150756836, 81.60513305664062, -76.70301818847656,
       42.02592849731445, -14.899847984313965, 3.238137722015381)


def horner(terms, y):
    total = y * terms[-1] + terms[-2]
    for term in terms[-3::-1]:
        total = total * y + term
    return total


def cos_sin(turns):
    r = turns - jnp.floor(turns + 0.5)
    y = r * r
    return horner(COS, y), r * horner(SIN, y)


def table_turns(steps, bins):
    return ((steps * bins) & (NT - 1)).astype(jnp.float32) * (1.0 / NT)


def spectrum_kernel(
    where_ref, signals_ref, bins_ref, gain_ref, damping_ref, damping_up_ref, stations_ref,
    send_ref, spec_ref, windowed, tables, hann, twiddle, later, group,
):
    sensors = spec_ref.shape[1]
    slices = send_ref.shape[0]
    q = pl.program_id(0)
    row = lax.broadcasted_iota(jnp.int32, (128, 128), 0)
    lane = lax.broadcasted_iota(jnp.int32, (128, 128), 1)

    @pl.when(q == 0)
    def _():
        times = (row * 128 + lane).astype(jnp.float32)
        hann[...] = 0.5 - 0.5 * cos_sin(times * (1.0 / NT))[0]
        for a in range(0, 128, 2):
            pair = [
                signals_ref[:, pl.ds(n * 128, 128)].astype(jnp.float32) * hann[n:n + 1, :]
                for n in (a, a + 1)
            ]
            windowed[pl.ds(a * sensors, 2 * sensors), :] = jnp.concatenate(
                pair, axis=0
            ).astype(jnp.bfloat16)
        groups = BLOCK // GROUP
        for g in range(groups):
            product = jnp.ones((1, damping_ref.shape[1]), jnp.float32)
            for k in range(g * GROUP + GROUP - 1, g * GROUP - 1, -1):
                later[k:k + 1, :] = product
                product = product * damping_ref[k:k + 1, :]
            group[g:g + 1, :] = product
            product = jnp.ones((1, damping_ref.shape[1]), jnp.float32)
            for k in range(g * GROUP, g * GROUP + GROUP):
                later[BLOCK + k:BLOCK + k + 1, :] = product
                product = product * damping_up_ref[k:k + 1, :]
            group[groups + g:groups + g + 1, :] = product
        stations = (stations_ref[...] - where_ref[1]).astype(jnp.float32)
        stations = jnp.concatenate([stations, stations + 64.0], axis=1)
        chosen = jnp.where(row.astype(jnp.float32) == stations, 1.0, 0.0).T
        gain = gain_ref[...].astype(jnp.float32)
        pick = functools.partial(
            jnp.dot, precision=lax.Precision.HIGHEST, preferred_element_type=jnp.float32
        )
        down = gain * pick(chosen[:64, :BLOCK], later[:BLOCK, :])
        up = gain * pick(chosen[64:, 64:64 + BLOCK], later[BLOCK:, :])
        values = jnp.concatenate([down, up], axis=0).T
        tables[:, :SLICE, :128] = values.reshape(slices, SLICE, 128)
        high = group[...].astype(jnp.bfloat16).astype(jnp.float32)
        rest = group[...] - high
        middle = rest.astype(jnp.bfloat16).astype(jnp.float32)
        fill = jnp.zeros((128 - 6 * groups, high.shape[1]), jnp.float32)
        terms = jnp.concatenate([high, middle, rest - middle, fill], axis=0).T
        tables[:, :SLICE, 128:] = terms.reshape(slices, SLICE, 128)
        tables[:, SLICE:, :] = jnp.zeros((slices, 64 - SLICE, 256), jnp.float32)
        for n in range(slices):
            tables[n, SLICE:SLICE + 8, :128] = jnp.broadcast_to(stations, (8, 128))

    bins = bins_ref[pl.ds(q, 1), :]
    c1, s1 = cos_sin(table_turns(row, bins))
    table = jnp.concatenate(
        [(c1 * (1 / 128)).astype(jnp.bfloat16), (s1 * (-1 / 128)).astype(jnp.bfloat16)], axis=1
    )
    twiddle[0], twiddle[1] = cos_sin(table_turns(row * 128, bins))
    sums = [[jnp.zeros((sensors, TILE), jnp.float32)] * 2 for _ in range(2)]
    few = 16
    for a in range(0, 128, few):
        part = jnp.dot(
            windowed[pl.ds(a * sensors, few * sensors), :], table, preferred_element_type=jnp.float32
        )
        for n in range(few):
            rows = slice(n * sensors, (n + 1) * sensors)
            re, im = part[rows, :TILE], part[rows, TILE:]
            c, s = twiddle[0, a + n:a + n + 1, :], twiddle[1, a + n:a + n + 1, :]
            turned = turn_back(c, s, re, im)
            sums[n % 2] = [x + y for x, y in zip(sums[n % 2], turned)]
    own = jnp.concatenate([x + y for x, y in zip(*sums)], axis=1)
    spec_ref[0] = own
    rows = pl.ds(pl.multiple_of(where_ref[0] * 8, 8), 8)
    for n in range(slices):
        send_ref[n, 0] = jnp.concatenate([own, tables[n, rows, :]], axis=0).astype(jnp.bfloat16)


def spectrum(where, signals, freq_bins, gain, damping, damping_up, stations, slices):
    sensors = signals.shape[0]
    tiles = freq_bins.shape[0] // TILE
    bins = freq_bins.reshape(tiles, TILE)
    stations = stations.reshape(1, -1)
    whole = lambda a: pl.BlockSpec(a.shape, lambda q: (0, 0))
    return pl.pallas_call(
        spectrum_kernel,
        grid=(tiles,),
        in_specs=[
            pl.BlockSpec(memory_space=pltpu.SMEM),
            whole(signals),
            whole(bins),
            whole(gain),
            whole(damping),
            whole(damping_up),
            whole(stations),
        ],
        out_specs=[
            pl.BlockSpec((slices, 1, 16, 2 * TILE), lambda q: (0, q, 0, 0)),
            pl.BlockSpec((1, sensors, 2 * TILE), lambda q: (q, 0, 0)),
        ],
        out_shape=[
            jax.ShapeDtypeStruct((slices, tiles, 16, 2 * TILE), jnp.bfloat16),
            jax.ShapeDtypeStruct((tiles, sensors, 2 * TILE), jnp.float32),
        ],
        scratch_shapes=[
            pltpu.VMEM((sensors * 128, 128), jnp.bfloat16),
            pltpu.VMEM((slices, 64, 2 * TILE), jnp.float32),
            pltpu.VMEM((128, 128), jnp.float32),
            pltpu.VMEM((2, 128, TILE), jnp.float32),
            pltpu.VMEM((2 * BLOCK, gain.shape[1]), jnp.float32),
            pltpu.VMEM((2 * BLOCK // GROUP, gain.shape[1]), jnp.float32),
        ],
        compiler_params=pltpu.CompilerParams(vmem_limit_bytes=56 * MIB),
        cost_estimate=pl.CostEstimate(flops=2 * 10**9, bytes_accessed=10**6, transcendentals=0),
        name="spectrum",
    )(where, signals, bins, gain, damping, damping_up, stations)


def inverse_kernel(bins_ref, after_ref, out_ref):
    del after_ref
    bins = bins_ref[:, 0:1]
    lane = lax.broadcasted_iota(jnp.int32, (TILE, 128), 1)
    c1, s1 = cos_sin(table_turns(lane, bins))
    c2, s2 = cos_sin(table_turns(lane * 128 + (NT - TOUT), bins))
    c2, s2 = c2 * (1 / 32), s2 * (1 / 32)
    for n in range(TOUT // 128):
        c, s = c2[:, n:n + 1], s2[:, n:n + 1]
        columns = pl.ds(n * 128, 128)
        out_ref[:TILE, columns] = (c1 * c - s1 * s).astype(jnp.bfloat16)
        out_ref[TILE:, columns] = (-s1 * c - c1 * s).astype(jnp.bfloat16)


def inverse_table(freq_bins, after):
    tiles = freq_bins.shape[0] // TILE
    bins = jnp.broadcast_to(freq_bins[:, None], (tiles * TILE, 128))
    return pl.pallas_call(
        inverse_kernel,
        grid=(tiles,),
        in_specs=[
            pl.BlockSpec((TILE, 128), lambda q: (q, 0)),
            pl.BlockSpec(memory_space=pl.ANY),
        ],
        out_specs=pl.BlockSpec((2 * TILE, TOUT), lambda q: (q, 0)),
        out_shape=jax.ShapeDtypeStruct((tiles * 2 * TILE, TOUT), jnp.bfloat16),
        compiler_params=pltpu.CompilerParams(vmem_limit_bytes=24 * MIB),
        cost_estimate=pl.CostEstimate(flops=4 * 10**9, bytes_accessed=5 * 10**6, transcendentals=0),
        name="inverse_table",
    )(bins, after)


def turn(c, s, re, im):
    return c * re - s * im, c * im + s * re


def turn_back(c, s, re, im):
    return c * re + s * im, c * im - s * re


def step(rate, turned, f_re, f_im):
    return rate * turned[0] + f_re, rate * turned[1] + f_im


def march_kernel(
    recv_ref, rot_ref, out_ref, done_ref, staged, sent, gains, places, specs, products
):
    done_ref[...] = jnp.zeros_like(done_ref)
    tiles = 8
    blocks = recv_ref.shape[0] // tiles
    groups = BLOCK // GROUP

    def unpack(block, unused):
        got = [recv_ref[block * tiles + p].astype(jnp.float32) for p in range(tiles)]
        both = jnp.concatenate([rows[8:, :128] for rows in got[:SLICE // 8]], axis=0)
        gains[block] = both
        places[block] = got[SLICE // 8][8:, :128]
        specs[block] = jnp.concatenate([rows[:8] for rows in got] * 2, axis=0).astype(jnp.bfloat16)
        terms = jnp.concatenate([rows[8:, 128:] for rows in got[:SLICE // 8]], axis=0)
        rates = terms[:, :2 * groups] + terms[:, 2 * groups:4 * groups]
        products[block, :, :2 * groups] = rates + terms[:, 4 * groups:6 * groups]
        return unused

    lax.fori_loop(0, blocks, unpack, 0, unroll=4)

    def forcing(block, direction, stations):
        gain, local = gains[block], places[block, 0:1]
        chosen = jnp.concatenate(
            [jnp.where(local == jnp.float32(k + 64 * direction), gain, 0.0) for k in stations], axis=0
        ).astype(jnp.bfloat16)
        return jnp.dot(chosen, specs[block], preferred_element_type=jnp.float32)

    down_of = [range(n * GROUP, n * GROUP + GROUP) for n in range(groups)]
    up_of = [range(BLOCK - 1 - n * GROUP, BLOCK - 1 - n * GROUP - GROUP, -1) for n in range(groups)]

    def across(turning, rate, near, far, state, forces):
        re, im = forces[:SLICE, :TILE], forces[:SLICE, TILE:]
        for i in range(1, GROUP):
            rows = slice(i * SLICE, (i + 1) * SLICE)
            re, im = turning(*near, re, im)
            re, im = re + forces[rows, :TILE], im + forces[rows, TILE:]
        return step(rate, turning(*far, *state), re, im)

    def body(b, carry):
        down, up = carry
        last = blocks - 1 - b
        near = rot_ref[0], rot_ref[1]
        far = rot_ref[2], rot_ref[3]
        down_rates, up_rates = products[b], products[last]
        for n in range(groups):
            here = b * groups + n
            staged[here, 0, :SLICE, :] = down[0].astype(jnp.bfloat16)
            staged[here, 0, SLICE:, :] = down[1].astype(jnp.bfloat16)
            m = groups - 1 - n
            here = last * groups + m
            staged[here, 1, :SLICE, :] = up[0].astype(jnp.bfloat16)
            staged[here, 1, SLICE:, :] = up[1].astype(jnp.bfloat16)
            down = across(
                turn_back, down_rates[:, n:n + 1], near, far, down, forcing(b, 0, down_of[n])
            )
            rate = up_rates[:, groups + m:groups + m + 1]
            up = across(turn, rate, near, far, up, forcing(last, 1, up_of[n]))
        for direction, block in ((0, b), (1, last)):
            part = pl.ds(block * groups, groups), direction
            pltpu.make_async_copy(staged.at[part], out_ref.at[part], sent).start()
        return down, up

    zero = jnp.zeros((SLICE, TILE), jnp.float32)
    lax.fori_loop(0, blocks, body, ((zero, zero), (zero, zero)))
    pltpu.make_async_copy(staged, out_ref, sent).wait()


def entering_states(recv, rot, blocks):
    shape = (blocks * BLOCK // GROUP, 2, 2 * SLICE, TILE)
    entering, done = pl.pallas_call(
        march_kernel,
        out_shape=[
            jax.ShapeDtypeStruct(shape, jnp.bfloat16),
            jax.ShapeDtypeStruct((8, 128), jnp.float32),
        ],
        in_specs=[pl.BlockSpec(memory_space=pltpu.VMEM)] * 2,
        out_specs=[pl.BlockSpec(memory_space=pl.ANY), pl.BlockSpec(memory_space=pltpu.VMEM)],
        scratch_shapes=[
            pltpu.VMEM(shape, jnp.bfloat16),
            pltpu.SemaphoreType.DMA,
            pltpu.VMEM((blocks, SLICE, 128), jnp.float32),
            pltpu.VMEM((blocks, 8, 128), jnp.float32),
            pltpu.VMEM((blocks, 128, 2 * TILE), jnp.bfloat16),
            pltpu.VMEM((blocks, SLICE, 128), jnp.float32),
        ],
        compiler_params=pltpu.CompilerParams(vmem_limit_bytes=56 * MIB),
        cost_estimate=pl.CostEstimate(flops=12 * 10**9, bytes_accessed=5 * 10**6, transcendentals=0),
        name="entering_states",
    )(recv, rot)
    return entering.reshape((-1,) + shape[2:]), done


TURN = GROUP + OWN
SKIP = TURN + 1


def local_kernel(
    gain_ref, rates_ref, spec_ref, omega_ref, after_ref, part_ref, rot_ref, done_ref, force, kept
):
    del after_ref
    done_ref[...] = jnp.zeros_like(done_ref)
    pair = force.shape[0]
    rates = rates_ref[0]

    def two(n, unused):
        for p in range(pair):
            q = n * pair + p
            force[p] = jnp.dot(gain_ref[0], spec_ref[q], preferred_element_type=jnp.float32)
        for p in range(pair):
            q = n * pair + p

            def forced(i):
                rows = pl.ds(i * SLICE, SLICE)
                return force[p, rows, :TILE], force[p, rows, TILE:]

            c, s = cos_sin(omega_ref[q, 0:1, :] * rates[:, TURN:TURN + 1])
            rot_ref[0, q, :SLICE, :] = c
            rot_ref[0, q, SLICE:, :] = s
            re, im = forced(GROUP - 1)
            kept[p, 0, 0], kept[p, 0, 1] = re, im
            for i in range(1, OWN):
                re, im = step(
                    rates[:, GROUP + i:GROUP + i + 1], turn_back(c, s, re, im),
                    *forced(GROUP - 1 - i),
                )
                kept[p, i, 0], kept[p, i, 1] = re, im
            re, im = forced(0)
            for i in range(1, GROUP):
                re, im = step(rates[:, i:i + 1], turn(c, s, re, im), *forced(i))
                if i >= GROUP - OWN:
                    n_own, n_near = i - (GROUP - OWN), GROUP - 1 - i
                    part_ref[0, q, n_own, :SLICE, :] = (re + kept[p, n_near, 0]).astype(jnp.bfloat16)
                    part_ref[0, q, n_own, SLICE:, :] = (im + kept[p, n_near, 1]).astype(jnp.bfloat16)
        return unused

    lax.fori_loop(0, spec_ref.shape[0] // pair, two, 0)


def local_states(gain, rates, spec, omega, after):
    slices, tiles = gain.shape[0], spec.shape[0]
    whole = lambda a: pl.BlockSpec(a.shape, lambda t: (0,) * a.ndim)
    return pl.pallas_call(
        local_kernel,
        grid=(slices,),
        in_specs=[
            pl.BlockSpec((1, GROUP * SLICE, 64), lambda t: (t, 0, 0)),
            pl.BlockSpec((1, SLICE, 128), lambda t: (t, 0, 0)),
            whole(spec),
            whole(omega),
            pl.BlockSpec(memory_space=pl.ANY),
        ],
        out_specs=[
            pl.BlockSpec((1, tiles, OWN, 2 * SLICE, TILE), lambda t: (t, 0, 0, 0, 0)),
            pl.BlockSpec((1, tiles, 2 * SLICE, TILE), lambda t: (t, 0, 0, 0)),
            pl.BlockSpec((8, 128), lambda t: (0, 0)),
        ],
        out_shape=[
            jax.ShapeDtypeStruct((slices, tiles, OWN, 2 * SLICE, TILE), jnp.bfloat16),
            jax.ShapeDtypeStruct((slices, tiles, 2 * SLICE, TILE), jnp.float32),
            jax.ShapeDtypeStruct((8, 128), jnp.float32),
        ],
        scratch_shapes=[
            pltpu.VMEM((2, GROUP * SLICE, 2 * TILE), jnp.float32),
            pltpu.VMEM((2, OWN, 2, SLICE, TILE), jnp.float32),
        ],
        compiler_params=pltpu.CompilerParams(vmem_limit_bytes=52 * MIB),
        cost_estimate=pl.CostEstimate(flops=20 * 10**9, bytes_accessed=20 * 10**6, transcendentals=0),
        name="local_states",
    )(gain, rates, spec, omega, after)


def estimate_kernel(
    core_ref, near_ref, far_ref, part_ref, rot_ref, rates_ref, inverse_ref, out_ref,
    even, odd, kept, inverse, ready,
):
    per, tiles = near_ref.shape[:2]
    height = per * SLICE
    index, last = pl.program_id(0), pl.num_programs(0) - 1
    core = core_ref[0]
    pieces = TOUT // 256

    def fill(state, q):
        lane = q * 2 * TILE
        for t in range(per):
            rates = rates_ref[t]
            c, s = rot_ref[t, q, :SLICE, :], rot_ref[t, q, SLICE:, :]
            re = near_ref[t, q, :SLICE, :].astype(jnp.float32)
            im = near_ref[t, q, SLICE:, :].astype(jnp.float32)
            for i in range(OWN):
                rate = rates[:, GROUP + i:GROUP + i + 1]
                re, im = turn_back(c, s, re, im)
                re, im = rate * re, rate * im
                kept[t, i, 0], kept[t, i, 1] = re, im
            c4, s4 = turn(c, s, c, s)
            c4, s4 = turn(c4, s4, c4, s4)
            re = far_ref[t, q, :SLICE, :].astype(jnp.float32)
            im = far_ref[t, q, SLICE:, :].astype(jnp.float32)
            re, im = turn(c4, s4, re, im)
            skip = rates[:, SKIP:SKIP + 1]
            re, im = skip * re, skip * im
            for i in range(OWN):
                rate = rates[:, GROUP - OWN + i:GROUP - OWN + i + 1]
                re, im = turn(c, s, re, im)
                re, im = rate * re, rate * im
                n = OWN - 1 - i
                rows = pl.ds(i * height + t * SLICE, SLICE)
                whole_re = re + kept[t, n, 0] + part_ref[t, q, i, :SLICE, :].astype(jnp.float32)
                whole_im = im + kept[t, n, 1] + part_ref[t, q, i, SLICE:, :].astype(jnp.float32)
                state[rows, lane:lane + TILE] = whole_re.astype(jnp.bfloat16)
                state[rows, lane + TILE:lane + 2 * TILE] = whole_im.astype(jnp.bfloat16)

    def multiply(state, n):
        columns = slice(n * 256, (n + 1) * 256)
        out = jnp.dot(state[...], inverse[:, columns], preferred_element_type=jnp.float32)
        for i in range(OWN):
            own = jnp.where(core == 0, OWN - 1 - i, i)
            out_ref[own, :, columns] = out[i * height:(i + 1) * height].astype(jnp.bfloat16)

    def both(filled, multiplied):
        for n in range(pieces):
            if multiplied is not None:
                multiply(multiplied, n)
            if filled is not None:
                for p in range(tiles // pieces):
                    fill(filled, n * (tiles // pieces) + p)

    fetch = pltpu.make_async_copy(inverse_ref, inverse, ready)
    inner = (index > 0) & (index < last)

    @pl.when(index == 0)
    def _():
        fetch.start()
        both(even, None)
        fetch.wait()

    pl.when(inner & (index % 2 == 1))(lambda: both(odd, even))
    pl.when(inner & (index % 2 == 0))(lambda: both(even, odd))
    pl.when(index == last)(lambda: both(None, odd))


def estimates(core, near, far, part, rot, rates, inverse):
    slices, tiles = near.shape[:2]
    per = 2
    steps = slices // per
    assert steps % 2 == 0
    here = lambda i: jnp.minimum(i, steps - 1)
    return pl.pallas_call(
        estimate_kernel,
        grid=(steps + 1,),
        in_specs=[
            pl.BlockSpec(memory_space=pltpu.SMEM),
            pl.BlockSpec((per, tiles, 2 * SLICE, TILE), lambda i: (here(i), 0, 0, 0)),
            pl.BlockSpec((per, tiles, 2 * SLICE, TILE), lambda i: (here(i), 0, 0, 0)),
            pl.BlockSpec((per, tiles, OWN, 2 * SLICE, TILE), lambda i: (here(i), 0, 0, 0, 0)),
            pl.BlockSpec((per, tiles, 2 * SLICE, TILE), lambda i: (here(i), 0, 0, 0)),
            pl.BlockSpec((per, SLICE, 128), lambda i: (here(i), 0, 0)),
            pl.BlockSpec(memory_space=pl.ANY),
        ],
        out_specs=pl.BlockSpec((OWN, per * SLICE, TOUT), lambda i: (0, jnp.maximum(i - 1, 0), 0)),
        out_shape=jax.ShapeDtypeStruct((OWN, slices * SLICE, TOUT), jnp.bfloat16),
        scratch_shapes=[
            pltpu.VMEM((OWN * per * SLICE, 2 * tiles * TILE), jnp.bfloat16),
            pltpu.VMEM((OWN * per * SLICE, 2 * tiles * TILE), jnp.bfloat16),
            pltpu.VMEM((per, OWN, 2, SLICE, TILE), jnp.float32),
            pltpu.VMEM(inverse.shape, inverse.dtype),
            pltpu.SemaphoreType.DMA,
        ],
        compiler_params=pltpu.CompilerParams(vmem_limit_bytes=40 * MIB),
        cost_estimate=pl.CostEstimate(flops=20 * 10**9, bytes_accessed=40 * 10**6, transcendentals=0),
        name="estimates",
    )(core, near, far, part, rot, rates, inverse)


def on_device(signals, freq_bins, sensor_station, gain, damping, damping_up, phase_speed):
    st, z, core = (lax.axis_index(axis) for axis in ALL)
    blocks = lax.axis_size("st")
    tiles = freq_bins.shape[0] // TILE
    sensors = sensor_station.shape[0]

    fq = (z * 2 + core).astype(jnp.int32)
    where = jnp.stack([fq, (st * BLOCK).astype(jnp.int32)])
    send, spec = spectrum(
        where, signals, freq_bins, gain, damping, damping_up, sensor_station, blocks
    )
    send = send.reshape((blocks * tiles,) + send.shape[2:])
    recv = lax.all_to_all(send, ALL, split_axis=0, concat_axis=0, tiled=True)
    spec_block = lax.all_gather(spec.astype(jnp.bfloat16), FQ)
    spec_block = spec_block.transpose(1, 0, 2, 3).reshape(tiles, sensors, 2 * TILE)

    omega = (freq_bins.astype(jnp.float32) / NT).reshape(tiles, 1, TILE)
    own_omega = lax.dynamic_index_in_dim(omega, fq, 0, keepdims=False)
    own_speed = lax.dynamic_slice_in_dim(phase_speed, st * SLICE, SLICE)
    theta = 2 * math.pi * own_omega * own_speed[:, None]
    past = theta * GROUP
    rot = jnp.stack([jnp.cos(theta), jnp.sin(theta), jnp.cos(past), jnp.sin(past)])
    recv, spec_block = lax.optimization_barrier((recv, spec_block))

    entering, done = entering_states(recv, rot, blocks)
    near = lax.all_to_all(entering, ALL, split_axis=0, concat_axis=0, tiled=True)
    damping, damping_up, gain, sensor_station, done = lax.optimization_barrier(
        (damping, damping_up, gain, sensor_station, done)
    )

    first = z * GROUP
    down = lax.dynamic_slice_in_dim(damping, first, GROUP)
    up = lax.dynamic_slice_in_dim(damping_up, first, GROUP)[::-1]
    far_rates = jnp.where(core == 0, up, down)
    near_rates = jnp.where(core == 0, down, up)[:OWN]
    speed = jnp.where(core == 0, phase_speed, -phase_speed)[None]
    skip = jnp.prod(far_rates[:GROUP - OWN], axis=0, keepdims=True)
    rates = jnp.concatenate([far_rates, near_rates, speed, skip], axis=0)
    rates = jnp.pad(rates, ((0, 128 - rates.shape[0]), (0, 0))).T.reshape(blocks, SLICE, 128)
    eight = lax.iota(jnp.int32, GROUP)
    far_order = first + jnp.where(core == 0, GROUP - 1 - eight, eight)
    local = sensor_station - st * BLOCK
    at = (local[None, :] == far_order[:, None])[None, :, None, :]
    own_gain = jnp.where(at, gain.T.reshape(blocks, 1, SLICE, sensors), 0)
    own_gain = own_gain.reshape(blocks, GROUP * SLICE, sensors)
    part, turns, done = local_states(
        own_gain, rates, spec_block, jnp.broadcast_to(omega, (tiles, 8, TILE)), done
    )
    inverse = inverse_table(freq_bins, done)
    near, part, turns = lax.optimization_barrier((near, part, turns))
    far = lax.ppermute(near, "core", [(0, 1), (1, 0)])
    shape = (blocks, tiles, 2 * SLICE, TILE)
    return estimates(
        core.reshape(1).astype(jnp.int32), near.reshape(shape), far.reshape(shape), part, turns,
        rates, inverse,
    )


def solution(mesh):
    torus = Mesh(mesh.devices.reshape(mesh.shape["st"], 4, 2), ALL)
    placed = (P(ALL, None), P(), P("st"), P("st", None), P("st", None), P("st", None), P())
    return jax.shard_map(
        on_device, mesh=torus, in_specs=placed, out_specs=P(ALL, None, None), check_vma=False
    )
```

```python
import functools
import math

import jax
import jax.numpy as jnp
from jax import lax
from jax.experimental import pallas as pl
from jax.experimental.pallas import tpu as pltpu
from jax.sharding import Mesh
from jax.sharding import PartitionSpec as P

NT = 16384
TOUT = 1024
BLOCK = 32
GROUP = 8
OWN = 4
TILE = 128
SLICE = 48
ALL = ("st", "z", "core")
FQ = ("z", "core")
MIB = 1 << 20

COS = (1.0, -19.739208221435547, 64.93939208984375, -85.45665740966797, 60.242130279541016,
       -26.4046688079834, 7.800131797790527, -1.4531123638153076)
SIN = (6.2831854820251465, -41.34170150756836, 81.60513305664062, -76.70301818847656,
       42.02592849731445, -14.899847984313965, 3.238137722015381)


def horner(terms, y):
    total = y * terms[-1] + terms[-2]
    for term in terms[-3::-1]:
        total = total * y + term
    return total


def cos_sin(turns):
    r = turns - jnp.floor(turns + 0.5)
    y = r * r
    return horner(COS, y), r * horner(SIN, y)


def table_turns(steps, bins):
    return ((steps * bins) & (NT - 1)).astype(jnp.float32) * (1.0 / NT)


def spectrum_kernel(
    where_ref, signals_ref, bins_ref, gain_ref, damping_ref, damping_up_ref, stations_ref,
    send_ref, spec_ref, windowed, tables, hann, twiddle, later, group,
):
    sensors = signals_ref.shape[0]
    slices = send_ref.shape[0]
    q = pl.program_id(0)
    row = lax.broadcasted_iota(jnp.int32, (128, 128), 0)
    lane = lax.broadcasted_iota(jnp.int32, (128, 128), 1)

    @pl.when(q == 0)
    def _():
        times = (row * 128 + lane).astype(jnp.float32)
        hann[...] = 0.5 - 0.5 * cos_sin(times * (1.0 / NT))[0]
        for a in range(0, 128, 2):
            pair = [
                signals_ref[:, pl.ds(n * 128, 128)].astype(jnp.float32) * hann[n:n + 1, :]
                for n in (a, a + 1)
            ]
            windowed[pl.ds(a * sensors, 2 * sensors), :] = jnp.concatenate(
                pair, axis=0
            ).astype(jnp.bfloat16)
        groups = BLOCK // GROUP
        for g in range(groups):
            product = jnp.ones((1, damping_ref.shape[1]), jnp.float32)
            for k in range(g * GROUP + GROUP - 1, g * GROUP - 1, -1):
                later[k:k + 1, :] = product
                product = product * damping_ref[k:k + 1, :]
            group[g:g + 1, :] = product
            product = jnp.ones((1, damping_ref.shape[1]), jnp.float32)
            for k in range(g * GROUP, g * GROUP + GROUP):
                later[BLOCK + k:BLOCK + k + 1, :] = product
                product = product * damping_up_ref[k:k + 1, :]
            group[groups + g:groups + g + 1, :] = product
        stations = (stations_ref[...] - where_ref[1]).astype(jnp.float32)
        stations = jnp.concatenate([stations, stations + 64.0], axis=1)
        chosen = jnp.where(row.astype(jnp.float32) == stations, 1.0, 0.0).T
        gain = gain_ref[...].astype(jnp.float32)
        pick = functools.partial(
            jnp.dot, precision=lax.Precision.HIGHEST, preferred_element_type=jnp.float32
        )
        down = gain * pick(chosen[:64, :BLOCK], later[:BLOCK, :])
        up = gain * pick(chosen[64:, 64:64 + BLOCK], later[BLOCK:, :])
        values = jnp.concatenate([down, up], axis=0).T
        tables[:, :SLICE, :128] = values.reshape(slices, SLICE, 128)
        high = group[...].astype(jnp.bfloat16).astype(jnp.float32)
        rest = group[...] - high
        middle = rest.astype(jnp.bfloat16).astype(jnp.float32)
        fill = jnp.zeros((128 - 6 * groups, high.shape[1]), jnp.float32)
        terms = jnp.concatenate([high, middle, rest - middle, fill], axis=0).T
        tables[:, :SLICE, 128:] = terms.reshape(slices, SLICE, 128)
        tables[:, SLICE:, :] = jnp.zeros((slices, 64 - SLICE, 256), jnp.float32)
        for n in range(slices):
            tables[n, SLICE:SLICE + 8, :128] = jnp.broadcast_to(stations, (8, 128))

    each = spec_ref.shape[0]
    for p in range(each):
        bins = bins_ref[pl.ds(q * each + p, 1), :]
        c1, s1 = cos_sin(table_turns(row, bins))
        table = jnp.concatenate(
            [(c1 * (1 / 128)).astype(jnp.bfloat16), (s1 * (-1 / 128)).astype(jnp.bfloat16)], axis=1
        )
        twiddle[p, 0], twiddle[p, 1] = cos_sin(table_turns(row * 128, bins))
        sums = [[jnp.zeros((sensors, TILE), jnp.float32)] * 2 for _ in range(2)]
        few = 16
        for a in range(0, 128, few):
            part = jnp.dot(
                windowed[pl.ds(a * sensors, few * sensors), :], table, preferred_element_type=jnp.float32
            )
            for n in range(few):
                rows = slice(n * sensors, (n + 1) * sensors)
                re, im = part[rows, :TILE], part[rows, TILE:]
                c, s = twiddle[p, 0, a + n:a + n + 1, :], twiddle[p, 1, a + n:a + n + 1, :]
                turned = turn_back(c, s, re, im)
                sums[n % 2] = [x + y for x, y in zip(sums[n % 2], turned)]
        both = [x + y for x, y in zip(*sums)]
        spec_ref[p] = jnp.concatenate(both, axis=0).astype(jnp.bfloat16)
        own = jnp.concatenate(both, axis=1)
        rows = pl.ds(pl.multiple_of(where_ref[0] * 8, 8), 8)
        for n in range(slices):
            send_ref[n, p] = jnp.concatenate([own, tables[n, rows, :]], axis=0).astype(jnp.bfloat16)


def spectrum(where, signals, freq_bins, gain, damping, damping_up, stations, slices):
    sensors = signals.shape[0]
    tiles = freq_bins.shape[0] // TILE
    each = 2
    bins = freq_bins.reshape(tiles, TILE)
    stations = stations.reshape(1, -1)
    whole = lambda a: pl.BlockSpec(a.shape, lambda q: (0, 0))
    return pl.pallas_call(
        spectrum_kernel,
        grid=(tiles // each,),
        in_specs=[
            pl.BlockSpec(memory_space=pltpu.SMEM),
            whole(signals),
            whole(bins),
            whole(gain),
            whole(damping),
            whole(damping_up),
            whole(stations),
        ],
        out_specs=[
            pl.BlockSpec((slices, each, 16, 2 * TILE), lambda q: (0, q, 0, 0)),
            pl.BlockSpec((each, 2 * sensors, TILE), lambda q: (q, 0, 0)),
        ],
        out_shape=[
            jax.ShapeDtypeStruct((slices, tiles, 16, 2 * TILE), jnp.bfloat16),
            jax.ShapeDtypeStruct((tiles, 2 * sensors, TILE), jnp.bfloat16),
        ],
        scratch_shapes=[
            pltpu.VMEM((sensors * 128, 128), jnp.bfloat16),
            pltpu.VMEM((slices, 64, 2 * TILE), jnp.float32),
            pltpu.VMEM((128, 128), jnp.float32),
            pltpu.VMEM((each, 2, 128, TILE), jnp.float32),
            pltpu.VMEM((2 * BLOCK, gain.shape[1]), jnp.float32),
            pltpu.VMEM((2 * BLOCK // GROUP, gain.shape[1]), jnp.float32),
        ],
        compiler_params=pltpu.CompilerParams(vmem_limit_bytes=56 * MIB),
        cost_estimate=pl.CostEstimate(flops=2 * 10**9, bytes_accessed=10**6, transcendentals=0),
        name="spectrum",
    )(where, signals, bins, gain, damping, damping_up, stations)


def inverse_kernel(bins_ref, after_ref, out_ref):
    del after_ref
    bins = bins_ref[:, 0:1]
    lane = lax.broadcasted_iota(jnp.int32, (TILE, 128), 1)
    c1, s1 = cos_sin(table_turns(lane, bins))
    c2, s2 = cos_sin(table_turns(lane * 128 + (NT - TOUT), bins))
    c2, s2 = c2 * (1 / 32), s2 * (1 / 32)
    for n in range(TOUT // 128):
        c, s = c2[:, n:n + 1], s2[:, n:n + 1]
        columns = pl.ds(n * 128, 128)
        out_ref[:TILE, columns] = (c1 * c - s1 * s).astype(jnp.bfloat16)
        out_ref[TILE:, columns] = (-s1 * c - c1 * s).astype(jnp.bfloat16)


def inverse_table(freq_bins, after):
    tiles = freq_bins.shape[0] // TILE
    bins = jnp.broadcast_to(freq_bins[:, None], (tiles * TILE, 128))
    return pl.pallas_call(
        inverse_kernel,
        grid=(tiles,),
        in_specs=[
            pl.BlockSpec((TILE, 128), lambda q: (q, 0)),
            pl.BlockSpec(memory_space=pl.ANY),
        ],
        out_specs=pl.BlockSpec((2 * TILE, TOUT), lambda q: (q, 0)),
        out_shape=jax.ShapeDtypeStruct((tiles * 2 * TILE, TOUT), jnp.bfloat16),
        compiler_params=pltpu.CompilerParams(vmem_limit_bytes=24 * MIB),
        cost_estimate=pl.CostEstimate(flops=4 * 10**9, bytes_accessed=5 * 10**6, transcendentals=0),
        name="inverse_table",
    )(bins, after)


def turn(c, s, re, im):
    return c * re - s * im, c * im + s * re


def turn_back(c, s, re, im):
    return c * re + s * im, c * im - s * re


def step(rate, turned, f_re, f_im):
    return rate * turned[0] + f_re, rate * turned[1] + f_im


def march_kernel(
    recv_ref, rot_ref, out_ref, done_ref, staged, sent, gains, places, specs, products
):
    done_ref[...] = jnp.zeros_like(done_ref)
    tiles = 8
    blocks = recv_ref.shape[0] // tiles
    groups = BLOCK // GROUP

    def unpack(block, unused):
        got = [recv_ref[block * tiles + p].astype(jnp.float32) for p in range(tiles)]
        both = jnp.concatenate([rows[8:, :128] for rows in got[:SLICE // 8]], axis=0)
        gains[block] = both
        places[block] = got[SLICE // 8][8:, :128]
        specs[block] = jnp.concatenate([rows[:8] for rows in got] * 2, axis=0).astype(jnp.bfloat16)
        terms = jnp.concatenate([rows[8:, 128:] for rows in got[:SLICE // 8]], axis=0)
        rates = terms[:, :2 * groups] + terms[:, 2 * groups:4 * groups]
        products[block, :, :2 * groups] = rates + terms[:, 4 * groups:6 * groups]
        return unused

    lax.fori_loop(0, blocks, unpack, 0, unroll=4)

    def forcing(block, direction, stations):
        gain, local = gains[block], places[block, 0:1]
        chosen = jnp.concatenate(
            [jnp.where(local == jnp.float32(k + 64 * direction), gain, 0.0) for k in stations], axis=0
        ).astype(jnp.bfloat16)
        return jnp.dot(chosen, specs[block], preferred_element_type=jnp.float32)

    down_of = [range(n * GROUP, n * GROUP + GROUP) for n in range(groups)]
    up_of = [range(BLOCK - 1 - n * GROUP, BLOCK - 1 - n * GROUP - GROUP, -1) for n in range(groups)]

    def across(turning, rate, near, far, state, forces):
        re, im = forces[:SLICE, :TILE], forces[:SLICE, TILE:]
        for i in range(1, GROUP):
            rows = slice(i * SLICE, (i + 1) * SLICE)
            re, im = turning(*near, re, im)
            re, im = re + forces[rows, :TILE], im + forces[rows, TILE:]
        return step(rate, turning(*far, *state), re, im)

    def body(b, carry):
        down, up = carry
        last = blocks - 1 - b
        near = rot_ref[0], rot_ref[1]
        far = rot_ref[2], rot_ref[3]
        down_rates, up_rates = products[b], products[last]
        for n in range(groups):
            here = b * groups + n
            staged[here, 0, :SLICE, :] = down[0].astype(jnp.bfloat16)
            staged[here, 0, SLICE:, :] = down[1].astype(jnp.bfloat16)
            m = groups - 1 - n
            here = last * groups + m
            staged[here, 1, :SLICE, :] = up[0].astype(jnp.bfloat16)
            staged[here, 1, SLICE:, :] = up[1].astype(jnp.bfloat16)
            down = across(
                turn_back, down_rates[:, n:n + 1], near, far, down, forcing(b, 0, down_of[n])
            )
            rate = up_rates[:, groups + m:groups + m + 1]
            up = across(turn, rate, near, far, up, forcing(last, 1, up_of[n]))
        for direction, block in ((0, b), (1, last)):
            part = pl.ds(block * groups, groups), direction
            pltpu.make_async_copy(staged.at[part], out_ref.at[part], sent).start()
        return down, up

    zero = jnp.zeros((SLICE, TILE), jnp.float32)
    lax.fori_loop(0, blocks, body, ((zero, zero), (zero, zero)))
    pltpu.make_async_copy(staged, out_ref, sent).wait()


def entering_states(recv, rot, blocks):
    shape = (blocks * BLOCK // GROUP, 2, 2 * SLICE, TILE)
    entering, done = pl.pallas_call(
        march_kernel,
        out_shape=[
            jax.ShapeDtypeStruct(shape, jnp.bfloat16),
            jax.ShapeDtypeStruct((8, 128), jnp.float32),
        ],
        in_specs=[pl.BlockSpec(memory_space=pltpu.VMEM)] * 2,
        out_specs=[pl.BlockSpec(memory_space=pl.ANY), pl.BlockSpec(memory_space=pltpu.VMEM)],
        scratch_shapes=[
            pltpu.VMEM(shape, jnp.bfloat16),
            pltpu.SemaphoreType.DMA,
            pltpu.VMEM((blocks, SLICE, 128), jnp.float32),
            pltpu.VMEM((blocks, 8, 128), jnp.float32),
            pltpu.VMEM((blocks, 128, 2 * TILE), jnp.bfloat16),
            pltpu.VMEM((blocks, SLICE, 128), jnp.float32),
        ],
        compiler_params=pltpu.CompilerParams(vmem_limit_bytes=56 * MIB),
        cost_estimate=pl.CostEstimate(flops=12 * 10**9, bytes_accessed=5 * 10**6, transcendentals=0),
        name="entering_states",
    )(recv, rot)
    return entering.reshape((-1,) + shape[2:]), done


TURN = GROUP + OWN
SKIP = TURN + 1


def local_kernel(
    gain_ref, rates_ref, spec_ref, omega_ref, after_ref, part_ref, rot_ref, done_ref, force, kept
):
    del after_ref
    done_ref[...] = jnp.zeros_like(done_ref)
    pair = force.shape[0]
    rates = rates_ref[0]

    def two(n, unused):
        for p in range(pair):
            q = n * pair + p
            force[p] = jnp.dot(gain_ref[0], spec_ref[q], preferred_element_type=jnp.float32)
        for p in range(pair):
            q = n * pair + p

            def forced(i):
                rows = pl.ds(i * SLICE, SLICE)
                return force[p, rows, :TILE], force[p, rows, TILE:]

            c, s = cos_sin(omega_ref[q, 0:1, :] * rates[:, TURN:TURN + 1])
            rot_ref[0, q, :SLICE, :] = c
            rot_ref[0, q, SLICE:, :] = s
            re, im = forced(GROUP - 1)
            kept[p, 0, 0], kept[p, 0, 1] = re, im
            for i in range(1, OWN):
                re, im = step(
                    rates[:, GROUP + i:GROUP + i + 1], turn_back(c, s, re, im),
                    *forced(GROUP - 1 - i),
                )
                kept[p, i, 0], kept[p, i, 1] = re, im
            re, im = forced(0)
            for i in range(1, GROUP):
                re, im = step(rates[:, i:i + 1], turn(c, s, re, im), *forced(i))
                if i >= GROUP - OWN:
                    n_own, n_near = i - (GROUP - OWN), GROUP - 1 - i
                    part_ref[0, q, n_own, :SLICE, :] = (re + kept[p, n_near, 0]).astype(jnp.bfloat16)
                    part_ref[0, q, n_own, SLICE:, :] = (im + kept[p, n_near, 1]).astype(jnp.bfloat16)
        return unused

    lax.fori_loop(0, spec_ref.shape[0] // pair, two, 0)


def local_states(gain, rates, spec, omega, after):
    slices, tiles = gain.shape[0], spec.shape[0]
    whole = lambda a: pl.BlockSpec(a.shape, lambda t: (0,) * a.ndim)
    return pl.pallas_call(
        local_kernel,
        grid=(slices,),
        in_specs=[
            pl.BlockSpec((1, GROUP * SLICE, 64), lambda t: (t, 0, 0)),
            pl.BlockSpec((1, SLICE, 128), lambda t: (t, 0, 0)),
            whole(spec),
            whole(omega),
            pl.BlockSpec(memory_space=pl.ANY),
        ],
        out_specs=[
            pl.BlockSpec((1, tiles, OWN, 2 * SLICE, TILE), lambda t: (t, 0, 0, 0, 0)),
            pl.BlockSpec((1, tiles, 2 * SLICE, TILE), lambda t: (t, 0, 0, 0)),
            pl.BlockSpec((8, 128), lambda t: (0, 0)),
        ],
        out_shape=[
            jax.ShapeDtypeStruct((slices, tiles, OWN, 2 * SLICE, TILE), jnp.bfloat16),
            jax.ShapeDtypeStruct((slices, tiles, 2 * SLICE, TILE), jnp.float32),
            jax.ShapeDtypeStruct((8, 128), jnp.float32),
        ],
        scratch_shapes=[
            pltpu.VMEM((2, GROUP * SLICE, 2 * TILE), jnp.float32),
            pltpu.VMEM((2, OWN, 2, SLICE, TILE), jnp.float32),
        ],
        compiler_params=pltpu.CompilerParams(vmem_limit_bytes=52 * MIB),
        cost_estimate=pl.CostEstimate(flops=20 * 10**9, bytes_accessed=20 * 10**6, transcendentals=0),
        name="local_states",
    )(gain, rates, spec, omega, after)


def estimate_kernel(
    core_ref, near_ref, far_ref, part_ref, rot_ref, rates_ref, inverse_ref, out_ref,
    even, odd, kept, inverse, ready,
):
    per, tiles = near_ref.shape[:2]
    height = per * SLICE
    index, last = pl.program_id(0), pl.num_programs(0) - 1
    core = core_ref[0]
    pieces = TOUT // 256

    def fill(state, q):
        lane = q * 2 * TILE
        for t in range(per):
            rates = rates_ref[t]
            c, s = rot_ref[t, q, :SLICE, :], rot_ref[t, q, SLICE:, :]
            re = near_ref[t, q, :SLICE, :].astype(jnp.float32)
            im = near_ref[t, q, SLICE:, :].astype(jnp.float32)
            for i in range(OWN):
                rate = rates[:, GROUP + i:GROUP + i + 1]
                re, im = turn_back(c, s, re, im)
                re, im = rate * re, rate * im
                kept[t, i, 0], kept[t, i, 1] = re, im
            c4, s4 = turn(c, s, c, s)
            c4, s4 = turn(c4, s4, c4, s4)
            re = far_ref[t, q, :SLICE, :].astype(jnp.float32)
            im = far_ref[t, q, SLICE:, :].astype(jnp.float32)
            re, im = turn(c4, s4, re, im)
            skip = rates[:, SKIP:SKIP + 1]
            re, im = skip * re, skip * im
            for i in range(OWN):
                rate = rates[:, GROUP - OWN + i:GROUP - OWN + i + 1]
                re, im = turn(c, s, re, im)
                re, im = rate * re, rate * im
                n = OWN - 1 - i
                rows = pl.ds(i * height + t * SLICE, SLICE)
                whole_re = re + kept[t, n, 0] + part_ref[t, q, i, :SLICE, :].astype(jnp.float32)
                whole_im = im + kept[t, n, 1] + part_ref[t, q, i, SLICE:, :].astype(jnp.float32)
                state[rows, lane:lane + TILE] = whole_re.astype(jnp.bfloat16)
                state[rows, lane + TILE:lane + 2 * TILE] = whole_im.astype(jnp.bfloat16)

    def multiply(state, n):
        columns = slice(n * 256, (n + 1) * 256)
        out = jnp.dot(state[...], inverse[:, columns], preferred_element_type=jnp.float32)
        for i in range(OWN):
            own = jnp.where(core == 0, OWN - 1 - i, i)
            out_ref[own, :, columns] = out[i * height:(i + 1) * height].astype(jnp.bfloat16)

    def both(filled, multiplied):
        for n in range(pieces):
            if multiplied is not None:
                multiply(multiplied, n)
            if filled is not None:
                for p in range(tiles // pieces):
                    fill(filled, n * (tiles // pieces) + p)

    fetch = pltpu.make_async_copy(inverse_ref, inverse, ready)
    inner = (index > 0) & (index < last)

    @pl.when(index == 0)
    def _():
        fetch.start()
        both(even, None)
        fetch.wait()

    pl.when(inner & (index % 2 == 1))(lambda: both(odd, even))
    pl.when(inner & (index % 2 == 0))(lambda: both(even, odd))
    pl.when(index == last)(lambda: both(None, odd))


def estimates(core, near, far, part, rot, rates, inverse):
    slices, tiles = near.shape[:2]
    per = 2
    steps = slices // per
    assert steps % 2 == 0
    here = lambda i: jnp.minimum(i, steps - 1)
    return pl.pallas_call(
        estimate_kernel,
        grid=(steps + 1,),
        in_specs=[
            pl.BlockSpec(memory_space=pltpu.SMEM),
            pl.BlockSpec((per, tiles, 2 * SLICE, TILE), lambda i: (here(i), 0, 0, 0)),
            pl.BlockSpec((per, tiles, 2 * SLICE, TILE), lambda i: (here(i), 0, 0, 0)),
            pl.BlockSpec((per, tiles, OWN, 2 * SLICE, TILE), lambda i: (here(i), 0, 0, 0, 0)),
            pl.BlockSpec((per, tiles, 2 * SLICE, TILE), lambda i: (here(i), 0, 0, 0)),
            pl.BlockSpec((per, SLICE, 128), lambda i: (here(i), 0, 0)),
            pl.BlockSpec(memory_space=pl.ANY),
        ],
        out_specs=pl.BlockSpec((OWN, per * SLICE, TOUT), lambda i: (0, jnp.maximum(i - 1, 0), 0)),
        out_shape=jax.ShapeDtypeStruct((OWN, slices * SLICE, TOUT), jnp.bfloat16),
        scratch_shapes=[
            pltpu.VMEM((OWN * per * SLICE, 2 * tiles * TILE), jnp.bfloat16),
            pltpu.VMEM((OWN * per * SLICE, 2 * tiles * TILE), jnp.bfloat16),
            pltpu.VMEM((per, OWN, 2, SLICE, TILE), jnp.float32),
            pltpu.VMEM(inverse.shape, inverse.dtype),
            pltpu.SemaphoreType.DMA,
        ],
        compiler_params=pltpu.CompilerParams(vmem_limit_bytes=40 * MIB),
        cost_estimate=pl.CostEstimate(flops=20 * 10**9, bytes_accessed=40 * 10**6, transcendentals=0),
        name="estimates",
    )(core, near, far, part, rot, rates, inverse)


def on_device(signals, freq_bins, sensor_station, gain, damping, damping_up, phase_speed):
    st, z, core = (lax.axis_index(axis) for axis in ALL)
    blocks = lax.axis_size("st")
    tiles = freq_bins.shape[0] // TILE
    sensors = sensor_station.shape[0]

    fq = (z * 2 + core).astype(jnp.int32)
    where = jnp.stack([fq, (st * BLOCK).astype(jnp.int32)])
    send, spec = spectrum(
        where, signals, freq_bins, gain, damping, damping_up, sensor_station, blocks
    )
    send = send.reshape((blocks * tiles,) + send.shape[2:])
    recv = lax.all_to_all(send, ALL, split_axis=0, concat_axis=0, tiled=True)
    recv, spec_block = lax.optimization_barrier((recv, lax.all_gather(spec, FQ)))
    spec_block = spec_block.reshape(tiles, tiles, 2, sensors // tiles, TILE)
    spec_block = spec_block.transpose(1, 0, 3, 2, 4).reshape(tiles, sensors, 2 * TILE)

    omega = (freq_bins.astype(jnp.float32) / NT).reshape(tiles, 1, TILE)
    own_omega = lax.dynamic_index_in_dim(omega, fq, 0, keepdims=False)
    own_speed = lax.dynamic_slice_in_dim(phase_speed, st * SLICE, SLICE)
    theta = 2 * math.pi * own_omega * own_speed[:, None]
    past = theta * GROUP
    rot = jnp.stack([jnp.cos(theta), jnp.sin(theta), jnp.cos(past), jnp.sin(past)])
    entering, done = entering_states(recv, rot, blocks)
    near = lax.all_to_all(entering, ALL, split_axis=0, concat_axis=0, tiled=True)
    damping, damping_up, gain, sensor_station, done = lax.optimization_barrier(
        (damping, damping_up, gain, sensor_station, done)
    )

    first = z * GROUP
    down = lax.dynamic_slice_in_dim(damping, first, GROUP)
    up = lax.dynamic_slice_in_dim(damping_up, first, GROUP)[::-1]
    far_rates = jnp.where(core == 0, up, down)
    near_rates = jnp.where(core == 0, down, up)[:OWN]
    speed = jnp.where(core == 0, phase_speed, -phase_speed)[None]
    skip = jnp.prod(far_rates[:GROUP - OWN], axis=0, keepdims=True)
    rates = jnp.concatenate([far_rates, near_rates, speed, skip], axis=0)
    rates = jnp.pad(rates, ((0, 128 - rates.shape[0]), (0, 0))).T.reshape(blocks, SLICE, 128)
    eight = lax.iota(jnp.int32, GROUP)
    far_order = first + jnp.where(core == 0, GROUP - 1 - eight, eight)
    local = sensor_station - st * BLOCK
    at = (local[None, :] == far_order[:, None])[None, :, None, :]
    own_gain = jnp.where(at, gain.T.reshape(blocks, 1, SLICE, sensors), 0)
    own_gain = own_gain.reshape(blocks, GROUP * SLICE, sensors)
    part, turns, done = local_states(
        own_gain, rates, spec_block, jnp.broadcast_to(omega, (tiles, 8, TILE)), done
    )
    inverse = inverse_table(freq_bins, done)
    near, part, turns = lax.optimization_barrier((near, part, turns))
    far = lax.ppermute(near, "core", [(0, 1), (1, 0)])
    shape = (blocks, tiles, 2 * SLICE, TILE)
    return estimates(
        core.reshape(1).astype(jnp.int32), near.reshape(shape), far.reshape(shape), part, turns,
        rates, inverse,
    )


def solution(mesh):
    torus = Mesh(mesh.devices.reshape(mesh.shape["st"], 4, 2), ALL)
    placed = (P(ALL, None), P(), P("st"), P("st", None), P("st", None), P("st", None), P())
    return jax.shard_map(
        on_device, mesh=torus, in_specs=placed, out_specs=P(ALL, None, None), check_vma=False
    )
```
